32 devices in a mesh: seq: 8 (over z, y), dp: 4 (over x, core).
Axes of the slice: x: 2, y: 2, z: 4, core: 2. Of those that a mesh axis runs over, the one named last changes fastest.
Arguments:
- queries: bfloat16 [4, 1024, 4096], P('dp', 'seq'), may hold values from -6 to 6
- key_vectors: bfloat16 [4, 1024, 4096], P('dp', 'seq'), may hold values from -6 to 6
- value_vectors: bfloat16 [4, 1024, 4096], P('dp', 'seq'), may hold values from -6 to 6
- out_grad: bfloat16 [4, 1024, 4096], P('dp', 'seq'), may hold values from -6 to 6
- norm_gain: float32 [4096], replicated, may hold values from 0.25 to 1.75
Outputs:
- query_grad: bfloat16 [4, 1024, 4096], P('dp', 'seq')
- key_grad: bfloat16 [4, 1024, 4096], P('dp', 'seq')
- value_grad: bfloat16 [4, 1024, 4096], P('dp', 'seq')
- gain_grad: float32 [4096], replicated
The draws below stay inside these ranges and needn't reach their ends.
All inputs are finite; a program needn't handle non-finite values.
Results may differ from the reference program's by a relative error of at most 0.006.
Values may be sent and summed in bfloat16 or wider, within the bound.
No kernel may reach another device: no remote copies, remote signals or barrier semaphores. Data moves between devices by JAX's collectives and lax.ppermute only.
A program may use at most 192 MiB of HBM per device.

```python
import math
import jax
import jax.numpy as jnp
from jax import lax

HEADS = 32
HEAD_DIM = 128
TOK_DEV = 128
SEQ_LEN = 1024
SLABS = 4


def block_scale(stream_key, extent, cuts, smallest, top_value):
    def one(position, shards_of):
        steps = jax.random.uniform(jax.random.fold_in(jax.random.fold_in(stream_key, 6), position), (shards_of,), jnp.float32, smallest / len(cuts), top_value / len(cuts))
        return jnp.repeat(jnp.exp(steps), extent[position] // shards_of).reshape((-1,) + (1,) * (len(extent) - position - 1))

    factor_of = one(*cuts[0])
    for cut in cuts[1:]:
        factor_of = factor_of * one(*cut)
    return factor_of


def noise(own_key, extent, deviation, most, pieces=(), dtype=jnp.bfloat16):
    drawn = jax.random.normal(own_key, extent, jnp.float32) * deviation
    if len(pieces) > 0:
        drawn = block_scale(own_key, extent, pieces, -0.22, 0.18) * drawn
    return jnp.clip(drawn, min=-most, max=most).astype(dtype)


def setup_inputs(seed: int = 0) -> dict:
    key_list = jax.random.split(jax.random.key(seed), 6)
    queries = noise(key_list[0], (SLABS, SEQ_LEN, HEADS * HEAD_DIM), 1.0, 6.0, ((0, 4), (1, 8)))
    key_vectors = noise(key_list[1], (SLABS, SEQ_LEN, HEADS * HEAD_DIM), 1.0, 6.0, ((0, 4), (1, 8)))
    value_vectors = noise(key_list[2], (SLABS, SEQ_LEN, HEADS * HEAD_DIM), 1.0, 6.0, ((0, 4), (1, 8)))
    out_grad = noise(key_list[3], (SLABS, SEQ_LEN, HEADS * HEAD_DIM), 1.0, 6.0, ((0, 4), (1, 8)))
    norm_gain = jnp.clip(1.0 + 0.15 * jax.random.normal(key_list[4], (HEADS * HEAD_DIM,), jnp.float32), 0.25, 1.75)
    return dict(queries=queries, key_vectors=key_vectors, value_vectors=value_vectors, out_grad=out_grad, norm_gain=norm_gain)


def widen(rounded):
    return lax.optimization_barrier(rounded).astype(jnp.float32)

def causal_scores(left, right):
    raw = jnp.einsum('thd,shd->hts', left.astype(jnp.float32), right.astype(jnp.float32))
    rows_count = left.shape[0]
    causal = lax.broadcasted_iota(jnp.int32, (rows_count, rows_count), 1) <= lax.broadcasted_iota(jnp.int32, (rows_count, rows_count), 0)
    return jnp.where(causal[None], raw, 0.0).astype(jnp.bfloat16)

def slab_pass(slab_inputs, gain_rows):
    blocks = SEQ_LEN // TOK_DEV
    shaped = tuple((item.reshape(blocks, TOK_DEV, HEADS, HEAD_DIM) for item in slab_inputs))

    def forward_block(carried, block_in):
        query_rows, key_rows, value_rows, grad_rows = block_in
        prefix_rounded = widen(carried.astype(jnp.bfloat16))
        scores = widen(causal_scores(query_rows, key_rows))
        attended = jnp.einsum('hts,shd->thd', scores, value_rows.astype(jnp.float32))
        attended = attended + jnp.einsum('thi,hij->thj', query_rows.astype(jnp.float32), prefix_rounded)
        inv_rms = lax.rsqrt(lax.optimization_barrier(jnp.mean(attended * attended, axis=-1, keepdims=True)) + 1e-05)
        normed = attended * inv_rms
        grad_wide = grad_rows.astype(jnp.float32)
        gain_part = lax.optimization_barrier(jnp.sum(grad_wide * normed, axis=0))
        scaled = grad_wide * gain_rows
        attn_grad = (inv_rms * (scaled - normed * lax.optimization_barrier(jnp.mean(scaled * normed, axis=-1, keepdims=True)))).astype(jnp.bfloat16)
        grad_scores = widen(causal_scores(attn_grad, value_rows))
        attn_wide = widen(attn_grad)
        query_grad = jnp.einsum('hts,shd->thd', grad_scores, key_rows.astype(jnp.float32))
        query_grad = query_grad + jnp.einsum('thj,hij->thi', attn_wide, prefix_rounded)
        block_state = jnp.einsum('shi,shj->hij', key_rows.astype(jnp.float32), value_rows.astype(jnp.float32))
        return (carried + block_state, (attn_grad, query_grad.astype(jnp.bfloat16), gain_part))
    start = jnp.zeros((HEADS, HEAD_DIM, HEAD_DIM), jnp.float32)
    unused, (attn_all, query_grad, gain_parts) = lax.scan(forward_block, start, shaped)

    def backward_block(carried, block_in):
        query_rows, key_rows, value_rows, attn_grad = block_in
        suffix_rounded = widen(carried.astype(jnp.bfloat16))
        scores = widen(causal_scores(query_rows, key_rows))
        grad_scores = widen(causal_scores(attn_grad, value_rows))
        attn_wide = attn_grad.astype(jnp.float32)
        query_wide = query_rows.astype(jnp.float32)
        key_wide = key_rows.astype(jnp.float32)
        key_grad = jnp.einsum('hts,thd->shd', grad_scores, query_wide)
        key_grad = key_grad + jnp.einsum('shj,hij->shi', value_rows.astype(jnp.float32), suffix_rounded)
        value_grad = jnp.einsum('hts,thd->shd', scores, attn_wide)
        value_grad = value_grad + jnp.einsum('shi,hij->shj', key_wide, suffix_rounded)
        back_state = jnp.einsum('thi,thj->hij', query_wide, attn_wide)
        return (carried + back_state, (key_grad.astype(jnp.bfloat16), value_grad.astype(jnp.bfloat16)))
    unused_back, (key_grad, value_grad) = lax.scan(backward_block, start, (shaped[0], shaped[1], shaped[2], attn_all), reverse=True)
    flat = (SEQ_LEN, HEADS * HEAD_DIM)
    return (query_grad.reshape(flat), key_grad.reshape(flat), value_grad.reshape(flat), lax.optimization_barrier(jnp.sum(gain_parts, axis=0)))

def reference(queries, key_vectors, value_vectors, out_grad, norm_gain):
    gain_rows = norm_gain.reshape(HEADS, HEAD_DIM)
    query_grad, key_grad, value_grad, gain_parts = lax.map(lambda slab_inputs: slab_pass(slab_inputs, gain_rows), (queries, key_vectors, value_vectors, out_grad))
    gain_grad = lax.optimization_barrier(jnp.sum(gain_parts, axis=0)) / math.sqrt(SLABS * SEQ_LEN)
    return (query_grad, key_grad, value_grad, gain_grad.reshape(HEADS * HEAD_DIM))
```

```python
import functools
import math

import jax
import jax.numpy as jnp
from jax import lax
from jax.experimental import pallas as pl
from jax.experimental.pallas import tpu as pltpu
from jax.sharding import PartitionSpec as P

HEAD_DIM = 128
CHUNKS = 1
F32 = jnp.float32
BF16 = jnp.bfloat16
VMEM = pltpu.VMEM


def dot(left, right, left_dim, right_dim):
    return lax.dot_general(
        left, right, (((left_dim,), (right_dim,)), ((), ())), preferred_element_type=F32
    )


def call(body, out_shape, args, flops, bytes_accessed):
    return pl.pallas_call(
        body,
        out_shape=out_shape,
        in_specs=[pl.BlockSpec(memory_space=pltpu.SMEM)]
        + [pl.BlockSpec(memory_space=VMEM)] * (len(args) - 1),
        out_specs=jax.tree.map(lambda _: pl.BlockSpec(memory_space=VMEM), out_shape),
        cost_estimate=pl.CostEstimate(
            flops=flops, bytes_accessed=bytes_accessed, transcendentals=0
        ),
        compiler_params=pltpu.CompilerParams(vmem_limit_bytes=32 * 2**20),
    )(*args)


def head_columns(place, chunk, slot, head, per_slot, group):
    owner = jnp.bitwise_xor(place, slot)
    first = chunk * per_slot * group + owner * per_slot + head
    return pl.ds(pl.multiple_of(first * HEAD_DIM, HEAD_DIM), HEAD_DIM)


def causal_mask(rows_count, transposed=False):
    rows = lax.broadcasted_iota(jnp.int32, (rows_count, rows_count), 0)
    columns = lax.broadcasted_iota(jnp.int32, (rows_count, rows_count), 1)
    return rows <= columns if transposed else columns <= rows


def make_states(chunk, group, per_slot, place_ref, left_ref, right_ref, *outs):
    place = place_ref[0]
    for slot in list(range(1, group)) + [0]:
        for head in range(per_slot):
            here = head_columns(place, chunk, slot, head, per_slot, group)
            state = dot(left_ref[:, here], right_ref[:, here], 0, 0)
            outs[slot][head] = state.astype(outs[slot].dtype)


def inside_blocks(
    chunk, group, per_slot, place_ref, query_ref, key_ref, value_ref, inside_ref, turned_ref
):
    mask = causal_mask(query_ref.shape[0])
    for at in range(group * per_slot):
        start = (chunk * group * per_slot + at) * HEAD_DIM
        here = pl.ds(start, HEAD_DIM)
        local = pl.ds(at * HEAD_DIM, HEAD_DIM)
        scores = jnp.where(mask, dot(query_ref[:, here], key_ref[:, here], 1, 1), 0.0)
        scores = scores.astype(BF16)
        inside_ref[:, local] = dot(scores, value_ref[:, here], 1, 0)
        turned_ref[:, local] = scores.T


def through_norm(
    chunk, group, per_slot, place_ref, query_ref, grad_ref, gain_ref, inside_ref, *refs
):
    prefixes, (attn_ref, part_ref), states = refs[:group], refs[group : group + 2], refs[group + 2 :]
    place = place_ref[0]
    for slot in list(range(1, group)) + [0]:
        for head in range(per_slot):
            here = head_columns(place, chunk, slot, head, per_slot, group)
            local = head_columns(place, 0, slot, head, per_slot, group)
            query = query_ref[:, here]
            attended = inside_ref[:, local] + dot(query, prefixes[slot][head], 1, 0)
            mean_square = jnp.mean(attended * attended, axis=-1, keepdims=True)
            inv_rms = lax.rsqrt(mean_square + 1e-05)
            normed = attended * inv_rms
            grad_wide = grad_ref[:, here].astype(F32)
            product = grad_wide * normed
            part_ref[:, local] = jnp.sum(product, axis=0, keepdims=True)
            gain = gain_ref[:, here]
            mean_product = jnp.mean(product * gain, axis=-1, keepdims=True)
            attn = (inv_rms * (grad_wide * gain - normed * mean_product)).astype(BF16)
            attn_ref[:, local] = attn
            state = dot(query, attn, 0, 0)
            states[slot][head] = state.astype(states[slot].dtype)


def query_side(
    chunk, group, per_slot, place_ref, key_ref, value_ref, attn_ref, *refs
):
    prefixes, (out_ref, turned_ref) = refs[:group], refs[group:]
    place = place_ref[0]
    mask = causal_mask(key_ref.shape[0])
    for slot in range(group):
        for head in range(per_slot):
            here = head_columns(place, chunk, slot, head, per_slot, group)
            local = head_columns(place, 0, slot, head, per_slot, group)
            attn = attn_ref[:, local]
            scores = jnp.where(mask, dot(attn, value_ref[:, here], 1, 1), 0.0).astype(BF16)
            turned_ref[:, local] = scores.T
            total = dot(scores, key_ref[:, here], 1, 0) + dot(attn, prefixes[slot][head], 1, 1)
            out_ref[:, local] = total.astype(BF16)


def key_side(
    chunk,
    group,
    per_slot,
    place_ref,
    query_ref,
    key_ref,
    value_ref,
    attn_ref,
    scores_ref,
    grad_scores_ref,
    *refs,
):
    suffixes, (key_out, value_out) = refs[:group], refs[group:]
    place = place_ref[0]
    for slot in list(range(1, group)) + [0]:
        for head in range(per_slot):
            here = head_columns(place, chunk, slot, head, per_slot, group)
            local = head_columns(place, 0, slot, head, per_slot, group)
            suffix = suffixes[slot][head]
            total = dot(grad_scores_ref[:, local], query_ref[:, here], 1, 0)
            total = total + dot(value_ref[:, here], suffix, 1, 1)
            key_out[:, local] = total.astype(BF16)
            total = dot(scores_ref[:, local], attn_ref[:, local], 1, 0)
            total = total + dot(key_ref[:, here], suffix, 1, 0)
            value_out[:, local] = total.astype(BF16)


def add_group(group, place_ref, *refs):
    parts, out_ref = refs[:group], refs[group]
    total = parts[0][...]
    for slot in range(1, group):
        total = total + parts[slot][...].astype(F32)
    out_ref[...] = total.astype(out_ref.dtype)


def scan_group(group, reverse, has_base, place_ref, *refs):
    parts, refs = refs[:group], refs[group:]
    place = place_ref[0]
    values = [part[...].astype(F32) for part in parts]
    if has_base:
        base, refs = refs[0][...].astype(F32), refs[1:]
        base = jnp.where(place_ref[1] == 1, base, 0.0)
    else:
        base = jnp.zeros_like(values[0])
    for slot in range(group):
        target = jnp.bitwise_xor(place, slot)
        total = base
        for other in range(group):
            if other == slot:
                continue
            source = jnp.bitwise_xor(place, other)
            counts = source > target if reverse else source < target
            total = total + jnp.where(counts, values[other], 0.0)
        refs[slot][...] = total.astype(BF16)


def swap(array, axis, bits):
    count = lax.axis_size(axis)
    return lax.ppermute(array, axis, [(i, i ^ bits) for i in range(count)])


def scan_states(states, group, reverse):
    count = lax.axis_size("seq")
    me = lax.axis_index("seq")
    place = me % group
    parts = [states[0]] + [swap(states[slot], "seq", slot) for slot in range(1, group)]
    shape = states[0].shape
    size = math.prod(shape)
    wide = jax.ShapeDtypeStruct(shape, F32)
    thin = jax.ShapeDtypeStruct(shape, BF16)
    steps = int(math.log2(count // group))
    base, is_base = None, jnp.int32(0)
    if steps:
        total = call(
            functools.partial(add_group, group),
            thin,
            [jnp.stack([place, place]).astype(jnp.int32)] + parts,
            4 * size,
            12 * size,
        )
        for step in range(steps):
            bits = group << step
            got = swap(total, "seq", bits)
            upper = (me & bits) != 0
            counts = jnp.logical_not(upper) if reverse else upper
            if steps == 1:
                base, is_base = got, counts.astype(jnp.int32)
            else:
                got = got.astype(F32)
                base = jnp.where(counts, got, 0.0) + (0.0 if base is None else base)
                total = (total.astype(F32) + got).astype(BF16)
                is_base = jnp.int32(1)
    scalars = jnp.stack([place.astype(jnp.int32), is_base])
    sends = call(
        functools.partial(scan_group, group, reverse, base is not None),
        [thin] * group,
        [scalars] + parts + ([] if base is None else [base]),
        16 * size,
        20 * size,
    )
    return [sends[0]] + [swap(sends[slot], "seq", slot) for slot in range(1, group)]


def sum_all(part):
    for axis in ("seq", "dp"):
        for step in range(int(math.log2(lax.axis_size(axis)))):
            part = part + swap(part, axis, 1 << step)
    return part


def local(queries, key_vectors, value_vectors, out_grad, norm_gain):
    rows, width = queries.shape[1:]
    heads = width // HEAD_DIM
    group = min(4, lax.axis_size("seq"))
    per_slot = heads // (group * CHUNKS)
    per_chunk = heads // CHUNKS
    q, k, v, g = (a.reshape(rows, width) for a in (queries, key_vectors, value_vectors, out_grad))
    gain = norm_gain.reshape(1, width)
    place = (lax.axis_index("seq") % group).astype(jnp.int32).reshape(1)
    cube = 2 * HEAD_DIM**3
    square = HEAD_DIM**2
    columns = per_chunk * HEAD_DIM
    state_types = [
        jax.ShapeDtypeStruct((per_slot, HEAD_DIM, HEAD_DIM), BF16 if slot else F32)
        for slot in range(group)
    ]
    tall = jax.ShapeDtypeStruct((rows, columns), BF16)
    tall_wide = jax.ShapeDtypeStruct((rows, columns), F32)
    sets = []
    for chunk in range(CHUNKS):
        fixed = (chunk, group, per_slot)
        states = call(
            functools.partial(make_states, *fixed),
            state_types,
            [place, k, v],
            per_chunk * cube,
            per_chunk * square * 8,
        )
        prefixes = scan_states(states, group, False)
        inside, scores = call(
            functools.partial(inside_blocks, *fixed),
            [tall_wide, tall],
            [place, q, k, v],
            per_chunk * cube * 2,
            per_chunk * square * 12,
        )
        attn, part, *back = call(
            functools.partial(through_norm, *fixed),
            [tall, jax.ShapeDtypeStruct((1, columns), F32)] + state_types,
            [place, q, g, gain, inside] + prefixes,
            per_chunk * cube * 2,
            per_chunk * square * 14,
        )
        suffixes = scan_states(back, group, True)
        query_grad, grad_scores = call(
            functools.partial(query_side, *fixed),
            [tall, tall],
            [place, k, v, attn] + prefixes,
            per_chunk * cube * 3,
            per_chunk * square * 12,
        )
        key_grad, value_grad = call(
            functools.partial(key_side, *fixed),
            [tall, tall],
            [place, q, k, v, attn, scores, grad_scores] + suffixes,
            per_chunk * cube * 4,
            per_chunk * square * 18,
        )
        sets.append((query_grad, key_grad, value_grad, part))
    query_grad, key_grad, value_grad, part = (
        jnp.concatenate(pieces, axis=1) if CHUNKS > 1 else pieces[0] for pieces in zip(*sets)
    )
    token_count = lax.axis_size("seq") * rows * lax.axis_size("dp")
    gain_grad = sum_all(part) / math.sqrt(token_count)
    return (
        query_grad.reshape(queries.shape),
        key_grad.reshape(queries.shape),
        value_grad.reshape(queries.shape),
        gain_grad.reshape(width),
    )


def solution(mesh):
    block = P("dp", "seq", None)
    return jax.shard_map(
        local,
        mesh=mesh,
        in_specs=(block, block, block, block, P()),
        out_specs=(block, block, block, P()),
        check_vma=False,
    )
```

```python
import functools
import math

import jax
import jax.numpy as jnp
from jax import lax
from jax.experimental import pallas as pl
from jax.experimental.pallas import tpu as pltpu
from jax.sharding import PartitionSpec as P

HEAD_DIM = 128
CHUNKS = 2
F32 = jnp.float32
BF16 = jnp.bfloat16
VMEM, HBM = pltpu.VMEM, pltpu.HBM
PLAN = ("add_prefix0", "score0", "add_prefix1", "scan_prefix0", "scan_prefix1", "norm0", "norm1", "add_suffix0", "gain", "query0", "gain", "add_suffix1", "scan_suffix0", "query1", "scan_suffix1", "key0", "key1",
)


def dot(left, right, left_dim, right_dim):
    return lax.dot_general(
        left, right, (((left_dim,), (right_dim,)), ((), ())), preferred_element_type=F32
    )


def call(body, name, outs, args, flops, nbytes, scratch=(), aliases=None, after=()):
    count = len(args)
    args = list(args) + list(after)
    arrays = [
        pltpu.with_memory_space_constraint(array, space) if space else array for array, space in args
    ]

    def kernel(*refs):
        body(*refs[:count], *refs[count + len(after) :])

    return pl.pallas_call(
        kernel,
        name=name,
        out_shape=[space(shape, dtype) for shape, dtype, space in outs],
        in_specs=[pl.BlockSpec(memory_space=space or VMEM) for _, space in args],
        out_specs=[pl.BlockSpec(memory_space=space) for _, _, space in outs],
        scratch_shapes=list(scratch),
        input_output_aliases=aliases or {},
        cost_estimate=pl.CostEstimate(
            flops=int(flops), bytes_accessed=int(nbytes), transcendentals=0
        ),
        compiler_params=pltpu.CompilerParams(vmem_limit_bytes=8 * 2**20),
    )(*arrays)


def place_in(group):
    me = lax.axis_index("seq")
    return lax.rem(me, group), lax.div(me, group)


def slot_columns(place, chunk, slot, per_slot, group, head=0, heads=None):
    owner = jnp.bitwise_xor(place, slot)
    heads = heads or per_slot
    start = ((chunk * group + owner) * per_slot + head) * HEAD_DIM
    return pl.ds(pl.multiple_of(start, heads * HEAD_DIM), heads * HEAD_DIM)


def head_columns(at):
    return pl.ds(at * HEAD_DIM, HEAD_DIM)


def head_rows(at):
    return pl.ds(at * HEAD_DIM, HEAD_DIM), slice(None)


def far_first(group):
    return list(range(group - 1, 0, -1)) + [0]


def load_slots(fixed, place, source, target, sems):
    chunk, group, per_slot = fixed
    width = per_slot * HEAD_DIM
    copies = {}
    for slot in far_first(group):
        copies[slot] = pltpu.make_async_copy(
            source.at[:, slot_columns(place, chunk, slot, per_slot, group)],
            target.at[:, pl.ds(slot * width, width)],
            sems.at[slot],
        )
        copies[slot].start()
    return copies


def store_heads(fixed, place, slot, head, heads, source, target, sem):
    chunk, group, per_slot = fixed
    copy = pltpu.make_async_copy(
        source.at[:, pl.ds((slot * per_slot + head) * HEAD_DIM, heads * HEAD_DIM)],
        target.at[:, slot_columns(place, chunk, slot, per_slot, group, head, heads)],
        sem,
    )
    copy.start()
    return copy


def causal_masks(rows_count):
    rows = lax.broadcasted_iota(jnp.int32, (rows_count, rows_count), 0)
    columns = lax.broadcasted_iota(jnp.int32, (rows_count, rows_count), 1)
    return columns <= rows, rows <= columns


def make_states(fixed, key_in, value_in, key_ref, value_ref, *refs):
    chunk, group, per_slot = fixed
    states, sems = refs[:group], refs[group]
    place, _ = place_in(group)
    keys = load_slots(fixed, place, key_in, key_ref, sems.at[0])
    values = load_slots(fixed, place, value_in, value_ref, sems.at[1])
    for slot in far_first(group):
        keys[slot].wait()
        values[slot].wait()
        for head in range(per_slot):
            here = head_columns(slot * per_slot + head)
            state = dot(key_ref[:, here], value_ref[:, here], 0, 0)
            states[slot][head_rows(head)] = state.astype(states[slot].dtype)


def make_scores(fixed, chunks, query_ref, *refs):
    _, group, per_slot = fixed
    place, _ = place_in(group)
    keys, scores, turned = (refs[i * chunks : (i + 1) * chunks] for i in range(3))
    mask, mask_turned = causal_masks(query_ref.shape[0])
    for c in range(chunks):
        for slot in far_first(group):
            for head in range(per_slot):
                here = head_columns(slot * per_slot + head)
                there = slot_columns(place, c, slot, per_slot, group, head, 1)
                query, key = query_ref[:, there], keys[c][:, here]
                scores[c][:, here] = jnp.where(mask, dot(query, key, 1, 1), 0.0).astype(BF16)
                turned[c][:, here] = jnp.where(mask_turned, dot(key, query, 1, 1), 0.0).astype(BF16)


def through_norm(fixed, has_part, query_ref, value_ref, grad_ref, gain_ref, scores_ref, *refs):
    chunk, group, per_slot = fixed
    prefixes, refs = refs[:group], refs[group:]
    if has_part:
        part_in, refs = refs[0], refs[1:]
    attn_ref, part_ref, *refs = refs
    states, attended_ref = refs[:group], refs[group]
    place, _ = place_in(group)
    if has_part:
        before = pl.ds(0, chunk * group * per_slot)
        part_ref[before] = part_in[before]
    each = [(slot, head) for slot in far_first(group) for head in range(per_slot)]
    for slot, head in each:
        here = head_columns(slot * per_slot + head)
        there = slot_columns(place, chunk, slot, per_slot, group, head, 1)
        left = jnp.concatenate([scores_ref[:, here], query_ref[:, there]], axis=1)
        right = jnp.concatenate([value_ref[:, here], prefixes[slot][head_rows(head)]], axis=0)
        attended_ref[:, here] = dot(left, right, 1, 0)
    for slot, head in each:
        here = head_columns(slot * per_slot + head)
        there = slot_columns(place, chunk, slot, per_slot, group, head, 1)
        attended = attended_ref[:, here]
        mean_square = jnp.mean(attended * attended, axis=-1, keepdims=True)
        inv_rms = lax.rsqrt(mean_square + 1e-05)
        normed = attended * inv_rms
        grad_wide = grad_ref[:, there].astype(F32)
        product = grad_wide * normed
        row = (chunk * group + jnp.bitwise_xor(place, slot)) * per_slot + head
        part_ref[pl.ds(row, 1)] = jnp.sum(product, axis=0, keepdims=True)
        gain = gain_ref[:, there]
        mean_product = jnp.mean(product * gain, axis=-1, keepdims=True)
        attn = inv_rms * (grad_wide * gain - normed * mean_product)
        attn_ref[:, here] = attn.astype(BF16)
    for slot, head in each:
        here = head_columns(slot * per_slot + head)
        there = slot_columns(place, chunk, slot, per_slot, group, head, 1)
        state = dot(query_ref[:, there], attn_ref[:, here], 0, 0)
        states[slot][head_rows(head)] = state.astype(states[slot].dtype)


def query_side(fixed, key_ref, value_ref, attn_ref, *refs):
    chunk, group, per_slot = fixed
    prefixes, (out_ref, turned_ref, scores_ref) = refs[:group], refs[group:]
    mask, mask_turned = causal_masks(key_ref.shape[0])
    for head in range(group * per_slot):
        here = head_columns(head)
        attn, value = attn_ref[:, here], value_ref[:, here]
        scores_ref[:, here] = jnp.where(mask, dot(attn, value, 1, 1), 0.0).astype(BF16)
        turned_ref[:, here] = jnp.where(mask_turned, dot(value, attn, 1, 1), 0.0).astype(BF16)
    for slot in range(group):
        for head in range(per_slot):
            here = head_columns(slot * per_slot + head)
            total = dot(scores_ref[:, here], key_ref[:, here], 1, 0)
            total = total + dot(attn_ref[:, here], prefixes[slot][head_rows(head)], 1, 1)
            out_ref[:, here] = total.astype(BF16)


def key_side(
    fixed, has_out, scale, query_ref, key_ref, value_ref, attn_ref, scores_ref, grad_scores_ref,
    query_grad_ref, *refs,
):
    chunk, group, per_slot = fixed
    suffixes, refs = refs[:group], refs[group:]
    if scale:
        part_ref, refs = refs[0], refs[1:]
    refs = refs[3 * has_out :]
    query_out, key_out, value_out, *refs = refs
    if scale:
        gain_out, refs = refs[0], refs[1:]
    key_buffer, value_buffer, sems, *refs = refs
    place, _ = place_in(group)
    copies = []

    def store(source, target, slot, head, heads):
        copies.append(
            store_heads(fixed, place, slot, head, heads, source, target, sems.at[len(copies)])
        )

    if scale:
        gain_buffer, gain_sem = refs
        first = per_slot * HEAD_DIM
        terms = [part_ref[...]] + [join(suffix, first) for suffix in suffixes[1:]]
        while len(terms) > 1:
            terms = [terms[i] + terms[i + 1] for i in range(0, len(terms), 2)]
        gain_buffer[...] = terms[0] * scale
        copy = pltpu.make_async_copy(gain_buffer, gain_out, gain_sem.at[0])
        copy.start()
    for slot in range(group):
        store(query_grad_ref, query_out, slot, 0, per_slot)
    for slot in range(group):
        for head in range(per_slot):
            here = head_columns(slot * per_slot + head)
            there = slot_columns(place, chunk, slot, per_slot, group, head, 1)
            suffix = suffixes[slot][head_rows(head)]
            total = dot(grad_scores_ref[:, here], query_ref[:, there], 1, 0)
            total = total + dot(value_ref[:, here], suffix, 1, 1)
            key_buffer[:, here] = total.astype(BF16)
            left = jnp.concatenate([scores_ref[:, here], key_ref[:, here]], axis=1)
            right = jnp.concatenate([attn_ref[:, here], suffix], axis=0)
            value_buffer[:, here] = dot(left, right, 1, 0).astype(BF16)
            if slot == group - 1:
                store(key_buffer, key_out, slot, head, 1)
                store(value_buffer, value_out, slot, head, 1)
        if slot < group - 1:
            store(key_buffer, key_out, slot, 0, per_slot)
            store(value_buffer, value_out, slot, 0, per_slot)
    if scale:
        copy.wait()
    for copy in copies:
        copy.wait()


def split(value):
    high = value.astype(BF16)
    return high, (value - high.astype(F32)).astype(BF16)


def join(ref, first):
    rows = (ref.shape[0] - first) // 2
    return ref[first : first + rows].astype(F32) + ref[first + rows : first + 2 * rows].astype(F32)


def put(ref, first, value):
    rows = value.shape[0]
    ref[first : first + rows], ref[first + rows : first + 2 * rows] = split(value)
    return join(ref, first)


HALF = HEAD_DIM // 2


def pieces(rows):
    return [(pl.ds(row, HALF), slice(None)) for row in range(0, rows, HALF)]


def add_group(group, carry, *refs):
    parts, out_ref = refs[:group], refs[-1]
    rows = parts[0].shape[0]
    for at in pieces(rows):
        total = parts[0][at]
        for slot in range(1, group):
            total = total + parts[slot][at].astype(F32)
        out_ref[at] = total.astype(out_ref.dtype)
    if carry:
        put(out_ref, rows, refs[group][...])


def scan_group(group, reverse, steps, carry, *refs):
    parts, refs = refs[:group], refs[group:]
    rows = parts[0].shape[0]
    if steps:
        base_ref, refs = refs[0], refs[1:]
    if carry:
        sent_ref, part_ref = refs[0], refs[-1]
        refs = refs[1:]
        both = join(sent_ref, rows) + join(base_ref, rows)
        for slot in range(1, group):
            part_ref[...] = put(refs[slot], rows, both)
    place, number = place_in(group)
    use_base = (number == (0 if reverse else 1)).astype(F32)
    counts = {}
    for slot in range(group):
        target = jnp.bitwise_xor(place, slot)
        for other in range(group):
            source = jnp.bitwise_xor(place, other)
            is_before = source > target if reverse else source < target
            counts[slot, other] = is_before.astype(F32)
    for at in pieces(rows):
        values = [part[at].astype(F32) for part in parts]
        if steps:
            base = base_ref[at].astype(F32)
            if steps == 1:
                base = base * use_base
        else:
            base = jnp.zeros_like(values[0])
        for slot in range(group):
            total = base
            for other in range(group):
                if other != slot:
                    total = total + values[other] * counts[slot, other]
            refs[slot][at] = total.astype(BF16)


def add_parts(scale, left_ref, right_ref, out_ref):
    out_ref[...] = (left_ref[...] + right_ref[...]) * scale


def swap(array, axis, bits):
    count = lax.axis_size(axis)
    return lax.ppermute(array, axis, [(i, i ^ bits) for i in range(count)])


def local(queries, key_vectors, value_vectors, out_grad, norm_gain):
    rows, width = queries.shape[1:]
    heads = width // HEAD_DIM
    count = lax.axis_size("seq")
    group = min(4, count)
    steps = int(math.log2(count // group))
    per_slot = heads // (group * CHUNKS)
    per_chunk = heads // CHUNKS
    k, v = ((a.reshape(rows, width), HBM) for a in (key_vectors, value_vectors))
    q, g = ((a.reshape(rows, width), None) for a in (queries, out_grad))
    gain = (norm_gain.reshape(1, width), None)
    me = lax.axis_index("seq")
    cube = 2 * HEAD_DIM**3
    square = HEAD_DIM**2
    columns = per_chunk * HEAD_DIM
    state_shape = (per_slot * HEAD_DIM, HEAD_DIM)
    size = per_slot * square
    thin_state = (state_shape, BF16, VMEM)
    state_outs = [(state_shape, F32, VMEM)] + [thin_state] * (group - 1)
    message = ((state_shape[0] + 2 * heads, HEAD_DIM), BF16, VMEM)
    part_type = ((heads, HEAD_DIM), F32, VMEM)
    carried = steps == 1 and group == 4
    tall = ((rows, columns), BF16, VMEM)
    result = ((rows, width), BF16, HBM)
    sems = pltpu.SemaphoreType.DMA

    def vm(arrays):
        return [(a, VMEM) for a in arrays]

    def spread(states):
        return [states[0]] + [swap(states[slot], "seq", slot) for slot in range(1, group)]

    def across(parts, reverse, name, after, gain_part=None):
        if not steps:
            return None, after
        carry = gain_part is not None
        (total,) = call(
            functools.partial(add_group, group, carry), name, [message if carry else thin_state],
            vm(parts + ([gain_part] if carry else [])), 4 * size, 12 * size, after=after,
        )
        done = [(total, VMEM)]
        if steps == 1:
            got = swap(total, "seq", group)
            return [got, total] if carry else [got], done
        base = None
        for step in range(steps):
            got = swap(total, "seq", group << step).astype(F32)
            upper = (me & (group << step)) != 0
            counts = jnp.logical_not(upper) if reverse else upper
            base = jnp.where(counts, got, 0.0) + (0.0 if base is None else base)
            total = (total.astype(F32) + got).astype(BF16)
        return [base], done

    def scan(parts, base, reverse, name, after, carry=False):
        out = call(
            functools.partial(scan_group, group, reverse, steps, carry), name,
            [thin_state] + [message if carry else thin_state] * (group - 1)
            + ([part_type] if carry else []),
            vm(parts + (base or [])), 16 * size, 20 * size, after=after,
        )
        return spread(out[:group]), [(out[0], VMEM)], out[-1]

    fixed = [(chunk, group, per_slot) for chunk in range(CHUNKS)]
    keys, values, parts, order = [], [], [], []
    for c in range(CHUNKS):
        key, value, *states = call(
            functools.partial(make_states, fixed[c]), f"make_states_{c}",
            [tall, tall] + state_outs, [k, v],
            per_chunk * cube, per_chunk * square * 10, [sems((2, group))], after=order,
        )
        keys.append(key)
        values.append(value)
        parts.append(spread(states))
        order = [(key, VMEM)]

    scores, turned = [], []
    prefixes, normed, back, query_grads = {}, {}, {}, {}
    grad_scores, suffixes, base = {}, {}, {}
    part, results = None, None

    def score(_):
        nonlocal order, scores, turned
        out = call(
            functools.partial(make_scores, fixed[0], CHUNKS), "make_scores", [tall] * (2 * CHUNKS),
            [q] + vm(keys), heads * cube * 2, heads * square * 12, after=order,
        )
        scores, turned = out[:CHUNKS], out[CHUNKS:]
        order = [(turned[0], VMEM)]

    def add_prefix(c):
        nonlocal order
        base[c], order = across(parts[c], False, f"add_prefix_{c}", order)

    def scan_prefix(c):
        nonlocal order
        prefixes[c], order, _ = scan(parts[c], base[c], False, f"scan_prefix_{c}", order)

    def add_suffix(c):
        nonlocal order
        carry = part if carried and c == CHUNKS - 1 else None
        base[c], order = across(back[c], True, f"add_suffix_{c}", order, carry)

    def scan_suffix(c):
        nonlocal order, part
        carry = carried and c == CHUNKS - 1
        suffixes[c], order, out = scan(back[c], base[c], True, f"scan_suffix_{c}", order, carry)
        if carry:
            part = out

    def norm(c):
        nonlocal order, part
        out = call(
            functools.partial(through_norm, fixed[c], part is not None), f"through_norm_{c}",
            [tall, part_type] + state_outs,
            [q, (values[c], VMEM), g, gain]
            + vm([scores[c]] + prefixes[c] + ([] if part is None else [part])),
            per_chunk * cube * 3, per_chunk * square * 14,
            [VMEM((rows, columns), F32)], after=order,
        )
        normed[c], part = out[:2]
        back[c] = spread(out[2:])
        order = [(normed[c], VMEM)]

    def query(c):
        nonlocal order
        query_grads[c], grad_scores[c] = call(
            functools.partial(query_side, fixed[c]), f"query_side_{c}", [tall, tall],
            vm([keys[c], values[c], normed[c]] + prefixes[c]),
            per_chunk * cube * 4, per_chunk * square * 12,
            [VMEM((rows, columns), BF16)], after=order,
        )
        order = [(grad_scores[c], VMEM)]

    def key(c):
        nonlocal order, results, part
        has_out = results is not None
        carry = carried and c == CHUNKS - 1
        args = [q] + vm(
            [keys[c], values[c], normed[c], turned[c], grad_scores[c], query_grads[c]]
            + suffixes[c] + ([part] if carry else [])
        )
        count_copies = 3 * group - 2 + 2 * per_slot
        scratch = [VMEM((rows, columns), BF16)] * 2 + [sems((count_copies,))]
        if carry:
            scratch += [VMEM(part_type[0], F32), sems((1,))]
        results = call(
            functools.partial(key_side, fixed[c], has_out, scale if carry else None),
            f"key_side_{c}", [result] * 3 + ([(part_type[0], F32, HBM)] if carry else []),
            args + [(out, HBM) for out in (results if has_out else [])],
            per_chunk * cube * 4, per_chunk * square * 20, scratch,
            {len(args) + i: i for i in range(3)} if has_out else None,
            after=() if has_out else order,
        )
        if carry:
            results, part = results[:3], results[3]
        order = [(results[0], HBM)]

    hops = [
        (axis, 1 << step)
        for axis in ("dp",) + (() if carried else ("seq",))
        for step in range(int(math.log2(lax.axis_size(axis))))
    ]
    scale = 1.0 / math.sqrt(count * rows * lax.axis_size("dp"))

    def gain_hop(at):
        nonlocal order, part
        axis, hop = hops[at]
        factor = 1.0 if carried or at < len(hops) - 1 else scale
        (part,) = call(
            functools.partial(add_parts, factor), f"add_gain_{at}", [part_type],
            vm([part, swap(part, axis, hop)]), width, 12 * width, after=order,
        )
        order = [(part, VMEM)]

    plan = PLAN
    stages = dict(
        add_prefix=add_prefix, scan_prefix=scan_prefix, add_suffix=add_suffix,
        scan_suffix=scan_suffix, score=score, norm=norm, query=query, key=key,
    )
    hop = 0
    for step in plan:
        if step == "gain":
            if hop < len(hops):
                gain_hop(hop)
                hop += 1
        else:
            stages[step[:-1]](int(step[-1]))
    while hop < len(hops):
        gain_hop(hop)
        hop += 1
    return (*(out.reshape(queries.shape) for out in results), part.reshape(width))


def solution(mesh):
    block = P("dp", "seq", None)
    return jax.shard_map(
        local,
        mesh=mesh,
        in_specs=(block, block, block, block, P()),
        out_specs=(block, block, block, P()),
        check_vma=False,
    )
```

```python
import functools
import math

import jax
import jax.numpy as jnp
from jax import lax
from jax.experimental import pallas as pl
from jax.experimental.pallas import tpu as pltpu
from jax.sharding import PartitionSpec as P

HEAD_DIM = 128
CHUNKS = 2
F32 = jnp.float32
BF16 = jnp.bfloat16
VMEM, HBM = pltpu.VMEM, pltpu.HBM
PLAN = ("add_prefix0", "score0", "add_prefix1", "scan_prefix0", "scan_prefix1", "norm0", "norm1", "add_suffix0", "query0", "gain", "add_suffix1", "scan_suffix0", "query1", "scan_suffix1", "key0", "total0", "key1",
)


def dot(left, right, left_dim, right_dim):
    return lax.dot_general(
        left, right, (((left_dim,), (right_dim,)), ((), ())), preferred_element_type=F32
    )


def call(body, name, outs, args, flops, nbytes, scratch=(), aliases=None, after=()):
    count = len(args)
    args = list(args) + list(after)
    arrays = [
        pltpu.with_memory_space_constraint(array, space) if space else array for array, space in args
    ]

    def kernel(*refs):
        body(*refs[:count], *refs[count + len(after) :])

    return pl.pallas_call(
        kernel,
        name=name,
        out_shape=[space(shape, dtype) for shape, dtype, space in outs],
        in_specs=[pl.BlockSpec(memory_space=space or VMEM) for _, space in args],
        out_specs=[pl.BlockSpec(memory_space=space) for _, _, space in outs],
        scratch_shapes=list(scratch),
        input_output_aliases=aliases or {},
        cost_estimate=pl.CostEstimate(
            flops=int(flops), bytes_accessed=int(nbytes), transcendentals=0
        ),
        compiler_params=pltpu.CompilerParams(vmem_limit_bytes=8 * 2**20),
    )(*arrays)


def place_in(group):
    me = lax.axis_index("seq")
    return lax.rem(me, group), lax.div(me, group)


def slot_columns(place, chunk, slot, per_slot, group, head=0, heads=None):
    owner = jnp.bitwise_xor(place, slot)
    heads = heads or per_slot
    start = ((chunk * group + owner) * per_slot + head) * HEAD_DIM
    return pl.ds(pl.multiple_of(start, heads * HEAD_DIM), heads * HEAD_DIM)


def head_columns(at):
    return pl.ds(at * HEAD_DIM, HEAD_DIM)


def head_rows(at):
    return pl.ds(at * HEAD_DIM, HEAD_DIM), slice(None)


def far_first(group):
    return list(range(group - 1, 0, -1)) + [0]


def load_slots(fixed, place, source, target, sems):
    chunk, group, per_slot = fixed
    width = per_slot * HEAD_DIM
    copies = {}
    for slot in far_first(group):
        copies[slot] = pltpu.make_async_copy(
            source.at[:, slot_columns(place, chunk, slot, per_slot, group)],
            target.at[:, pl.ds(slot * width, width)],
            sems.at[slot],
        )
        copies[slot].start()
    return copies


def store_heads(fixed, place, slot, head, heads, source, target, sem):
    chunk, group, per_slot = fixed
    copy = pltpu.make_async_copy(
        source.at[:, pl.ds((slot * per_slot + head) * HEAD_DIM, heads * HEAD_DIM)],
        target.at[:, slot_columns(place, chunk, slot, per_slot, group, head, heads)],
        sem,
    )
    copy.start()
    return copy


def causal_masks(rows_count):
    rows = lax.broadcasted_iota(jnp.int32, (rows_count, rows_count), 0)
    columns = lax.broadcasted_iota(jnp.int32, (rows_count, rows_count), 1)
    return columns <= rows, rows <= columns


def make_states(fixed, key_in, value_in, key_ref, value_ref, *refs):
    chunk, group, per_slot = fixed
    states, sems = refs[:group], refs[group]
    place, _ = place_in(group)
    keys = load_slots(fixed, place, key_in, key_ref, sems.at[0])
    values = load_slots(fixed, place, value_in, value_ref, sems.at[1])
    for slot in far_first(group):
        keys[slot].wait()
        values[slot].wait()
        for head in range(per_slot):
            here = head_columns(slot * per_slot + head)
            state = dot(key_ref[:, here], value_ref[:, here], 0, 0)
            states[slot][head_rows(head)] = state.astype(states[slot].dtype)


def make_scores(fixed, chunks, query_ref, *refs):
    _, group, per_slot = fixed
    place, _ = place_in(group)
    keys, scores, turned = (refs[i * chunks : (i + 1) * chunks] for i in range(3))
    mask, mask_turned = causal_masks(query_ref.shape[0])
    for c in range(chunks):
        for slot in far_first(group):
            for head in range(per_slot):
                here = head_columns(slot * per_slot + head)
                there = slot_columns(place, c, slot, per_slot, group, head, 1)
                query, key = query_ref[:, there], keys[c][:, here]
                scores[c][:, here] = jnp.where(mask, dot(query, key, 1, 1), 0.0).astype(BF16)
                turned[c][:, here] = jnp.where(mask_turned, dot(key, query, 1, 1), 0.0).astype(BF16)


def through_norm(fixed, has_part, query_ref, value_ref, grad_ref, gain_ref, scores_ref, *refs):
    chunk, group, per_slot = fixed
    prefixes, refs = refs[:group], refs[group:]
    if has_part:
        part_in, refs = refs[0], refs[1:]
    attn_ref, part_ref, *refs = refs
    states, attended_ref = refs[:group], refs[group]
    place, _ = place_in(group)
    if has_part:
        before = pl.ds(0, chunk * group * per_slot)
        part_ref[before] = part_in[before]
    each = [(slot, head) for slot in far_first(group) for head in range(per_slot)]
    for slot, head in each:
        here = head_columns(slot * per_slot + head)
        there = slot_columns(place, chunk, slot, per_slot, group, head, 1)
        left = jnp.concatenate([scores_ref[:, here], query_ref[:, there]], axis=1)
        right = jnp.concatenate([value_ref[:, here], prefixes[slot][head_rows(head)]], axis=0)
        attended_ref[:, here] = dot(left, right, 1, 0)
    for slot, head in each:
        here = head_columns(slot * per_slot + head)
        there = slot_columns(place, chunk, slot, per_slot, group, head, 1)
        attended = attended_ref[:, here]
        mean_square = jnp.mean(attended * attended, axis=-1, keepdims=True)
        inv_rms = lax.rsqrt(mean_square + 1e-05)
        normed = attended * inv_rms
        grad_wide = grad_ref[:, there].astype(F32)
        product = grad_wide * normed
        row = (chunk * group + jnp.bitwise_xor(place, slot)) * per_slot + head
        part_ref[pl.ds(row, 1)] = jnp.sum(product, axis=0, keepdims=True)
        gain = gain_ref[:, there]
        mean_product = jnp.mean(product * gain, axis=-1, keepdims=True)
        attn = inv_rms * (grad_wide * gain - normed * mean_product)
        attn_ref[:, here] = attn.astype(BF16)
    for slot, head in each:
        here = head_columns(slot * per_slot + head)
        there = slot_columns(place, chunk, slot, per_slot, group, head, 1)
        state = dot(query_ref[:, there], attn_ref[:, here], 0, 0)
        states[slot][head_rows(head)] = state.astype(states[slot].dtype)


def query_side(fixed, key_ref, value_ref, attn_ref, *refs):
    chunk, group, per_slot = fixed
    prefixes, (out_ref, turned_ref, scores_ref) = refs[:group], refs[group:]
    mask, mask_turned = causal_masks(key_ref.shape[0])
    for head in range(group * per_slot):
        here = head_columns(head)
        attn, value = attn_ref[:, here], value_ref[:, here]
        scores_ref[:, here] = jnp.where(mask, dot(attn, value, 1, 1), 0.0).astype(BF16)
        turned_ref[:, here] = jnp.where(mask_turned, dot(value, attn, 1, 1), 0.0).astype(BF16)
    for slot in range(group):
        for head in range(per_slot):
            here = head_columns(slot * per_slot + head)
            total = dot(scores_ref[:, here], key_ref[:, here], 1, 0)
            total = total + dot(attn_ref[:, here], prefixes[slot][head_rows(head)], 1, 1)
            out_ref[:, here] = total.astype(BF16)


def key_side(
    fixed, has_out, query_ref, key_ref, value_ref, attn_ref, scores_ref, grad_scores_ref,
    query_grad_ref, *refs,
):
    chunk, group, per_slot = fixed
    suffixes, refs = refs[:group], refs[group + 3 * has_out :]
    query_out, key_out, value_out, key_buffer, value_buffer, sems = refs
    place, _ = place_in(group)
    copies = []

    def store(source, target, slot, head, heads):
        copies.append(
            store_heads(fixed, place, slot, head, heads, source, target, sems.at[len(copies)])
        )

    for slot in range(group):
        store(query_grad_ref, query_out, slot, 0, per_slot)
    for slot in range(group):
        for head in range(per_slot):
            here = head_columns(slot * per_slot + head)
            there = slot_columns(place, chunk, slot, per_slot, group, head, 1)
            suffix = suffixes[slot][head_rows(head)]
            total = dot(grad_scores_ref[:, here], query_ref[:, there], 1, 0)
            total = total + dot(value_ref[:, here], suffix, 1, 1)
            key_buffer[:, here] = total.astype(BF16)
            left = jnp.concatenate([scores_ref[:, here], key_ref[:, here]], axis=1)
            right = jnp.concatenate([attn_ref[:, here], suffix], axis=0)
            value_buffer[:, here] = dot(left, right, 1, 0).astype(BF16)
            if slot == group - 1:
                store(key_buffer, key_out, slot, head, 1)
                store(value_buffer, value_out, slot, head, 1)
        if slot < group - 1:
            store(key_buffer, key_out, slot, 0, per_slot)
            store(value_buffer, value_out, slot, 0, per_slot)
    for copy in copies:
        copy.wait()


def split(value):
    high = value.astype(BF16)
    return high, (value - high.astype(F32)).astype(BF16)


def join(ref, first):
    rows = (ref.shape[0] - first) // 2
    return ref[first : first + rows].astype(F32) + ref[first + rows : first + 2 * rows].astype(F32)


def put(ref, first, value):
    rows = value.shape[0]
    ref[first : first + rows], ref[first + rows : first + 2 * rows] = split(value)
    return join(ref, first)


HALF = HEAD_DIM // 2


def pieces(rows):
    return [(pl.ds(row, HALF), slice(None)) for row in range(0, rows, HALF)]


def add_group(group, carry, *refs):
    parts, out_ref = refs[:group], refs[-1]
    rows = parts[0].shape[0]
    for at in pieces(rows):
        total = parts[0][at]
        for slot in range(1, group):
            total = total + parts[slot][at].astype(F32)
        out_ref[at] = total.astype(out_ref.dtype)
    if carry:
        put(out_ref, rows, refs[group][...])


def scan_group(group, reverse, steps, carry, *refs):
    parts, refs = refs[:group], refs[group:]
    rows = parts[0].shape[0]
    if steps:
        base_ref, refs = refs[0], refs[1:]
    if carry:
        sent_ref, part_ref = refs[0], refs[-1]
        refs = refs[1:]
        both = join(sent_ref, rows) + join(base_ref, rows)
        for slot in range(1, group):
            part_ref[...] = put(refs[slot], rows, both)
    place, number = place_in(group)
    use_base = (number == (0 if reverse else 1)).astype(F32)
    counts = {}
    for slot in range(group):
        target = jnp.bitwise_xor(place, slot)
        for other in range(group):
            source = jnp.bitwise_xor(place, other)
            is_before = source > target if reverse else source < target
            counts[slot, other] = is_before.astype(F32)
    for at in pieces(rows):
        values = [part[at].astype(F32) for part in parts]
        if steps:
            base = base_ref[at].astype(F32)
            if steps == 1:
                base = base * use_base
        else:
            base = jnp.zeros_like(values[0])
        for slot in range(group):
            total = base
            for other in range(group):
                if other != slot:
                    total = total + values[other] * counts[slot, other]
            refs[slot][at] = total.astype(BF16)


def add_parts(left_ref, right_ref, out_ref):
    out_ref[...] = left_ref[...] + right_ref[...]


def sum_messages(part_ref, *refs):
    messages, out_ref = refs[:-1], refs[-1]
    first = messages[0].shape[0] - 2 * part_ref.shape[0]
    terms = [part_ref[...]] + [join(message, first) for message in messages]
    while len(terms) > 1:
        terms = [terms[i] + terms[i + 1] for i in range(0, len(terms), 2)]
    out_ref[...] = terms[0]


def finish_parts(scale, left_ref, right_ref, out_ref, buffer, sem):
    buffer[...] = (left_ref[...] + right_ref[...]) * scale
    copy = pltpu.make_async_copy(buffer, out_ref, sem.at[0])
    copy.start()
    copy.wait()


def swap(array, axis, bits):
    count = lax.axis_size(axis)
    return lax.ppermute(array, axis, [(i, i ^ bits) for i in range(count)])


def local(queries, key_vectors, value_vectors, out_grad, norm_gain):
    rows, width = queries.shape[1:]
    heads = width // HEAD_DIM
    count = lax.axis_size("seq")
    group = min(4, count)
    steps = int(math.log2(count // group))
    per_slot = heads // (group * CHUNKS)
    per_chunk = heads // CHUNKS
    k, v = ((a.reshape(rows, width), HBM) for a in (key_vectors, value_vectors))
    q, g = ((a.reshape(rows, width), None) for a in (queries, out_grad))
    gain = (norm_gain.reshape(1, width), None)
    me = lax.axis_index("seq")
    cube = 2 * HEAD_DIM**3
    square = HEAD_DIM**2
    columns = per_chunk * HEAD_DIM
    state_shape = (per_slot * HEAD_DIM, HEAD_DIM)
    size = per_slot * square
    thin_state = (state_shape, BF16, VMEM)
    state_outs = [(state_shape, F32, VMEM)] + [thin_state] * (group - 1)
    message = ((state_shape[0] + 2 * heads, HEAD_DIM), BF16, VMEM)
    part_type = ((heads, HEAD_DIM), F32, VMEM)
    carried = steps == 1 and group == 4
    tall = ((rows, columns), BF16, VMEM)
    result = ((rows, width), BF16, HBM)
    sems = pltpu.SemaphoreType.DMA

    def vm(arrays):
        return [(a, VMEM) for a in arrays]

    def spread(states):
        return [states[0]] + [swap(states[slot], "seq", slot) for slot in range(1, group)]

    def across(parts, reverse, name, after, gain_part=None):
        if not steps:
            return None, after
        carry = gain_part is not None
        (total,) = call(
            functools.partial(add_group, group, carry), name, [message if carry else thin_state],
            vm(parts + ([gain_part] if carry else [])), 4 * size, 12 * size, after=after,
        )
        done = [(total, VMEM)]
        if steps == 1:
            got = swap(total, "seq", group)
            return [got, total] if carry else [got], done
        base = None
        for step in range(steps):
            got = swap(total, "seq", group << step).astype(F32)
            upper = (me & (group << step)) != 0
            counts = jnp.logical_not(upper) if reverse else upper
            base = jnp.where(counts, got, 0.0) + (0.0 if base is None else base)
            total = (total.astype(F32) + got).astype(BF16)
        return [base], done

    def scan(parts, base, reverse, name, after, carry=False):
        out = call(
            functools.partial(scan_group, group, reverse, steps, carry), name,
            [thin_state] + [message if carry else thin_state] * (group - 1)
            + ([part_type] if carry else []),
            vm(parts + (base or [])), 16 * size, 20 * size, after=after,
        )
        return spread(out[:group]), [(out[0], VMEM)], out[-1]

    fixed = [(chunk, group, per_slot) for chunk in range(CHUNKS)]
    keys, values, parts, order = [], [], [], []
    for c in range(CHUNKS):
        key, value, *states = call(
            functools.partial(make_states, fixed[c]), f"make_states_{c}",
            [tall, tall] + state_outs, [k, v],
            per_chunk * cube, per_chunk * square * 10, [sems((2, group))], after=order,
        )
        keys.append(key)
        values.append(value)
        parts.append(spread(states))
        order = [(key, VMEM)]

    scores, turned = [], []
    prefixes, normed, back, query_grads = {}, {}, {}, {}
    grad_scores, suffixes, base = {}, {}, {}
    part, results = None, None

    def score(_):
        nonlocal order, scores, turned
        out = call(
            functools.partial(make_scores, fixed[0], CHUNKS), "make_scores", [tall] * (2 * CHUNKS),
            [q] + vm(keys), heads * cube * 2, heads * square * 12, after=order,
        )
        scores, turned = out[:CHUNKS], out[CHUNKS:]
        order = [(turned[0], VMEM)]

    def add_prefix(c):
        nonlocal order
        base[c], order = across(parts[c], False, f"add_prefix_{c}", order)

    def scan_prefix(c):
        nonlocal order
        prefixes[c], order, _ = scan(parts[c], base[c], False, f"scan_prefix_{c}", order)

    def add_suffix(c):
        nonlocal order
        carry = part if carried and c == CHUNKS - 1 else None
        base[c], order = across(back[c], True, f"add_suffix_{c}", order, carry)

    def scan_suffix(c):
        nonlocal order, part
        carry = carried and c == CHUNKS - 1
        suffixes[c], order, out = scan(back[c], base[c], True, f"scan_suffix_{c}", order, carry)
        if carry:
            part = out

    def norm(c):
        nonlocal order, part
        out = call(
            functools.partial(through_norm, fixed[c], part is not None), f"through_norm_{c}",
            [tall, part_type] + state_outs,
            [q, (values[c], VMEM), g, gain]
            + vm([scores[c]] + prefixes[c] + ([] if part is None else [part])),
            per_chunk * cube * 3, per_chunk * square * 14,
            [VMEM((rows, columns), F32)], after=order,
        )
        normed[c], part = out[:2]
        back[c] = spread(out[2:])
        order = [(normed[c], VMEM)]

    def query(c):
        nonlocal order
        query_grads[c], grad_scores[c] = call(
            functools.partial(query_side, fixed[c]), f"query_side_{c}", [tall, tall],
            vm([keys[c], values[c], normed[c]] + prefixes[c]),
            per_chunk * cube * 4, per_chunk * square * 12,
            [VMEM((rows, columns), BF16)], after=order,
        )
        order = [(grad_scores[c], VMEM)]

    def key(c):
        nonlocal order, results
        has_out = results is not None
        args = [q] + vm(
            [keys[c], values[c], normed[c], turned[c], grad_scores[c], query_grads[c]] + suffixes[c]
        )
        results = call(
            functools.partial(key_side, fixed[c], has_out), f"key_side_{c}", [result] * 3,
            args + [(out, HBM) for out in (results if has_out else [])],
            per_chunk * cube * 4, per_chunk * square * 20,
            [VMEM((rows, columns), BF16)] * 2 + [sems((3 * group - 2 + 2 * per_slot,))],
            {len(args) + i: i for i in range(3)} if has_out else None,
            after=() if has_out else order,
        )
        order = [(results[0], HBM)]

    def bits_of(axis):
        return [(axis, 1 << step) for step in range(int(math.log2(lax.axis_size(axis))))]

    hops = bits_of("dp")[1:] + ([] if carried else bits_of("seq")) + bits_of("dp")[:1]
    scale = 1.0 / math.sqrt(count * rows * lax.axis_size("dp"))

    def gain_hop(at):
        nonlocal order, part
        axis, hop = hops[at]
        args = vm([part, swap(part, axis, hop)])
        if at < len(hops) - 1:
            (part,) = call(
                add_parts, f"add_gain_{at}", [part_type], args, width, 12 * width, after=order
            )
            order = [(part, VMEM)]
        else:
            (part,) = call(
                functools.partial(finish_parts, scale), "finish_gain", [(part_type[0], F32, HBM)],
                args, width, 12 * width, [VMEM(part_type[0], F32), sems((1,))],
            )

    def gain_sum(_):
        nonlocal part
        if carried:
            (part,) = call(
                sum_messages, "sum_gain", [part_type], vm([part] + suffixes[CHUNKS - 1][1:]),
                width, 12 * width,
            )

    plan = PLAN
    stages = dict(
        add_prefix=add_prefix, scan_prefix=scan_prefix, add_suffix=add_suffix,
        scan_suffix=scan_suffix, score=score, total=gain_sum, norm=norm, query=query, key=key,
    )
    hop = 0
    for step in plan:
        if step == "gain":
            if hop < len(hops) - 1:
                gain_hop(hop)
                hop += 1
        else:
            stages[step[:-1]](int(step[-1]))
    while hop < len(hops):
        gain_hop(hop)
        hop += 1
    return (*(out.reshape(queries.shape) for out in results), part.reshape(width))


def solution(mesh):
    block = P("dp", "seq", None)
    return jax.shard_map(
        local,
        mesh=mesh,
        in_specs=(block, block, block, block, P()),
        out_specs=(block, block, block, P()),
        check_vma=False,
    )
```

```python
import functools
import math

import jax
import jax.numpy as jnp
from jax import lax
from jax.experimental import pallas as pl
from jax.experimental.pallas import tpu as pltpu
from jax.sharding import PartitionSpec as P

HEAD_DIM = 128
CHUNKS = 2
F32 = jnp.float32
BF16 = jnp.bfloat16
VMEM, HBM = pltpu.VMEM, pltpu.HBM
PLAN = ("add_prefix0", "score0", "add_prefix1", "scan_prefix0", "scan_prefix1", "norm0", "norm1", "add_suffix0", "query0", "gain", "add_suffix1", "scan_suffix0", "scan_suffix1", "query1", "key0", "total0", "key1",
)


def dot(left, right, left_dim, right_dim):
    return lax.dot_general(
        left, right, (((left_dim,), (right_dim,)), ((), ())), preferred_element_type=F32
    )


def call(body, name, outs, args, flops, nbytes, scratch=(), aliases=None, after=()):
    count = len(args)
    args = list(args) + list(after)
    arrays = [
        pltpu.with_memory_space_constraint(array, space) if space else array for array, space in args
    ]

    def kernel(*refs):
        body(*refs[:count], *refs[count + len(after) :])

    return pl.pallas_call(
        kernel,
        name=name,
        out_shape=[space(shape, dtype) for shape, dtype, space in outs],
        in_specs=[pl.BlockSpec(memory_space=space or VMEM) for _, space in args],
        out_specs=[pl.BlockSpec(memory_space=space) for _, _, space in outs],
        scratch_shapes=list(scratch),
        input_output_aliases=aliases or {},
        cost_estimate=pl.CostEstimate(
            flops=int(flops), bytes_accessed=int(nbytes), transcendentals=0
        ),
        compiler_params=pltpu.CompilerParams(vmem_limit_bytes=8 * 2**20),
    )(*arrays)


def place_in(group):
    me = lax.axis_index("seq")
    return lax.rem(me, group), lax.div(me, group)


def slot_columns(place, chunk, slot, per_slot, group, head=0, heads=None):
    owner = jnp.bitwise_xor(place, slot)
    heads = heads or per_slot
    start = ((chunk * group + owner) * per_slot + head) * HEAD_DIM
    return pl.ds(pl.multiple_of(start, heads * HEAD_DIM), heads * HEAD_DIM)


def head_columns(at):
    return pl.ds(at * HEAD_DIM, HEAD_DIM)


def head_rows(at):
    return pl.ds(at * HEAD_DIM, HEAD_DIM), slice(None)


def far_first(group):
    return list(range(group - 1, 0, -1)) + [0]


def load_slots(fixed, place, source, target, sems):
    chunk, group, per_slot = fixed
    width = per_slot * HEAD_DIM
    copies = {}
    for slot in far_first(group):
        copies[slot] = pltpu.make_async_copy(
            source.at[:, slot_columns(place, chunk, slot, per_slot, group)],
            target.at[:, pl.ds(slot * width, width)],
            sems.at[slot],
        )
        copies[slot].start()
    return copies


def store_heads(fixed, place, slot, head, heads, source, target, sem):
    chunk, group, per_slot = fixed
    copy = pltpu.make_async_copy(
        source.at[:, pl.ds((slot * per_slot + head) * HEAD_DIM, heads * HEAD_DIM)],
        target.at[:, slot_columns(place, chunk, slot, per_slot, group, head, heads)],
        sem,
    )
    copy.start()
    return copy


def causal_masks(rows_count):
    rows = lax.broadcasted_iota(jnp.int32, (rows_count, rows_count), 0)
    columns = lax.broadcasted_iota(jnp.int32, (rows_count, rows_count), 1)
    return columns <= rows, rows <= columns


def make_states(fixed, key_in, value_in, key_ref, value_ref, *refs):
    chunk, group, per_slot = fixed
    states, sems = refs[:group], refs[group]
    place, _ = place_in(group)
    if chunk:
        keys = load_slots(fixed, place, key_in, key_ref, sems.at[0])
        values = load_slots(fixed, place, value_in, value_ref, sems.at[1])
    else:
        copies = [
            pltpu.make_async_copy(
                source.at[:, pl.ds(0, buffer.shape[1])], buffer, sems.at[at, 0]
            )
            for at, (source, buffer) in enumerate(zip((key_in, value_in), refs[group + 1 :]))
        ]
        for copy in copies:
            copy.start()
        for copy in copies:
            copy.wait()
    for slot in far_first(group):
        if chunk:
            keys[slot].wait()
            values[slot].wait()
        for head in range(per_slot):
            here = head_columns(slot * per_slot + head)
            if chunk:
                key, value = key_ref[:, here], value_ref[:, here]
            else:
                near = slot_columns(place, 0, slot, per_slot, group, head, 1)
                key, value = (buffer[:, near] for buffer in refs[group + 1 :])
                key_ref[:, here], value_ref[:, here] = key, value
            state = dot(key, value, 0, 0)
            states[slot][head_rows(head)] = state.astype(states[slot].dtype)


def make_scores(fixed, chunks, query_ref, *refs):
    _, group, per_slot = fixed
    place, _ = place_in(group)
    keys, scores, turned = (refs[i * chunks : (i + 1) * chunks] for i in range(3))
    mask, mask_turned = causal_masks(query_ref.shape[0])
    for c in range(chunks):
        for slot in far_first(group):
            for head in range(per_slot):
                here = head_columns(slot * per_slot + head)
                there = slot_columns(place, c, slot, per_slot, group, head, 1)
                query, key = query_ref[:, there], keys[c][:, here]
                scores[c][:, here] = jnp.where(mask, dot(query, key, 1, 1), 0.0).astype(BF16)
                turned[c][:, here] = jnp.where(mask_turned, dot(key, query, 1, 1), 0.0).astype(BF16)


def through_norm(fixed, has_part, query_ref, value_ref, grad_ref, gain_ref, scores_ref, *refs):
    chunk, group, per_slot = fixed
    prefixes, refs = refs[:group], refs[group:]
    if has_part:
        part_in, refs = refs[0], refs[1:]
    attn_ref, part_ref, *refs = refs
    states, attended_ref = refs[:group], refs[group]
    place, _ = place_in(group)
    if has_part:
        before = pl.ds(0, chunk * group * per_slot)
        part_ref[before] = part_in[before]
    each = [(slot, head) for slot in far_first(group) for head in range(per_slot)]
    for slot, head in each:
        here = head_columns(slot * per_slot + head)
        there = slot_columns(place, chunk, slot, per_slot, group, head, 1)
        left = jnp.concatenate([scores_ref[:, here], query_ref[:, there]], axis=1)
        right = jnp.concatenate([value_ref[:, here], prefixes[slot][head_rows(head)]], axis=0)
        attended_ref[:, here] = dot(left, right, 1, 0)
    for slot, head in each:
        here = head_columns(slot * per_slot + head)
        there = slot_columns(place, chunk, slot, per_slot, group, head, 1)
        attended = attended_ref[:, here]
        mean_square = jnp.mean(attended * attended, axis=-1, keepdims=True)
        inv_rms = lax.rsqrt(mean_square + 1e-05)
        normed = attended * inv_rms
        grad_wide = grad_ref[:, there].astype(F32)
        product = grad_wide * normed
        row = (chunk * group + jnp.bitwise_xor(place, slot)) * per_slot + head
        part_ref[pl.ds(row, 1)] = jnp.sum(product, axis=0, keepdims=True)
        gain = gain_ref[:, there]
        mean_product = jnp.mean(product * gain, axis=-1, keepdims=True)
        attn = inv_rms * (grad_wide * gain - normed * mean_product)
        attn_ref[:, here] = attn.astype(BF16)
    for slot, head in each:
        here = head_columns(slot * per_slot + head)
        there = slot_columns(place, chunk, slot, per_slot, group, head, 1)
        state = dot(query_ref[:, there], attn_ref[:, here], 0, 0)
        states[slot][head_rows(head)] = state.astype(states[slot].dtype)


def query_side(fixed, query_ref, key_ref, value_ref, attn_ref, scores_turned_ref, *refs):
    chunk, group, per_slot = fixed
    prefixes, refs = refs[:group], refs[group:]
    out_ref, key_part_ref, value_part_ref, turned_ref, scores_ref = refs
    place, _ = place_in(group)
    mask, mask_turned = causal_masks(key_ref.shape[0])
    for head in range(group * per_slot):
        here = head_columns(head)
        attn, value = attn_ref[:, here], value_ref[:, here]
        scores_ref[:, here] = jnp.where(mask, dot(attn, value, 1, 1), 0.0).astype(BF16)
        turned_ref[:, here] = jnp.where(mask_turned, dot(value, attn, 1, 1), 0.0).astype(BF16)
    for slot in range(group):
        for head in range(per_slot):
            here = head_columns(slot * per_slot + head)
            total = dot(scores_ref[:, here], key_ref[:, here], 1, 0)
            total = total + dot(attn_ref[:, here], prefixes[slot][head_rows(head)], 1, 1)
            out_ref[:, here] = total.astype(BF16)
            there = slot_columns(place, chunk, slot, per_slot, group, head, 1)
            key_part_ref[:, here] = dot(turned_ref[:, here], query_ref[:, there], 1, 0)
            value_part_ref[:, here] = dot(scores_turned_ref[:, here], attn_ref[:, here], 1, 0)


def key_side(
    fixed, has_out, key_ref, value_ref, key_part_ref, value_part_ref, query_grad_ref, *refs
):
    chunk, group, per_slot = fixed
    suffixes, refs = refs[:group], refs[group + 3 * has_out :]
    query_out, key_out, value_out, key_buffer, value_buffer, sems = refs
    place, _ = place_in(group)
    copies = []

    def store(source, target, slot, head, heads):
        copies.append(
            store_heads(fixed, place, slot, head, heads, source, target, sems.at[len(copies)])
        )

    for slot in range(group):
        store(query_grad_ref, query_out, slot, 0, per_slot)
    for slot in range(group):
        for head in range(per_slot):
            here = head_columns(slot * per_slot + head)
            suffix = suffixes[slot][head_rows(head)]
            total = key_part_ref[:, here] + dot(value_ref[:, here], suffix, 1, 1)
            key_buffer[:, here] = total.astype(BF16)
            total = value_part_ref[:, here] + dot(key_ref[:, here], suffix, 1, 0)
            value_buffer[:, here] = total.astype(BF16)
            if slot == group - 1:
                store(key_buffer, key_out, slot, head, 1)
                store(value_buffer, value_out, slot, head, 1)
        if slot < group - 1:
            store(key_buffer, key_out, slot, 0, per_slot)
            store(value_buffer, value_out, slot, 0, per_slot)
    for copy in copies:
        copy.wait()


def split(value):
    high = value.astype(BF16)
    return high, (value - high.astype(F32)).astype(BF16)


def join(ref, first):
    rows = (ref.shape[0] - first) // 2
    return ref[first : first + rows].astype(F32) + ref[first + rows : first + 2 * rows].astype(F32)


def put(ref, first, value):
    rows = value.shape[0]
    ref[first : first + rows], ref[first + rows : first + 2 * rows] = split(value)
    return join(ref, first)


HALF = HEAD_DIM // 2


def pieces(rows):
    return [(pl.ds(row, HALF), slice(None)) for row in range(0, rows, HALF)]


def add_group(group, carry, *refs):
    parts, out_ref = refs[:group], refs[-1]
    rows = parts[0].shape[0]
    for at in pieces(rows):
        total = parts[0][at]
        for slot in range(1, group):
            total = total + parts[slot][at].astype(F32)
        out_ref[at] = total.astype(out_ref.dtype)
    if carry:
        put(out_ref, rows, refs[group][...])


def scan_group(group, reverse, steps, carry, *refs):
    parts, refs = refs[:group], refs[group:]
    rows = parts[0].shape[0]
    if steps:
        base_ref, refs = refs[0], refs[1:]
    if carry:
        sent_ref, part_ref = refs[0], refs[-1]
        refs = refs[1:]
        both = join(sent_ref, rows) + join(base_ref, rows)
        for slot in range(1, group):
            part_ref[...] = put(refs[slot], rows, both)
    place, number = place_in(group)
    use_base = (number == (0 if reverse else 1)).astype(F32)
    counts = {}
    for slot in range(group):
        target = jnp.bitwise_xor(place, slot)
        for other in range(group):
            source = jnp.bitwise_xor(place, other)
            is_before = source > target if reverse else source < target
            counts[slot, other] = is_before.astype(F32)
    for at in pieces(rows):
        values = [part[at].astype(F32) for part in parts]
        if steps:
            base = base_ref[at].astype(F32)
            if steps == 1:
                base = base * use_base
        else:
            base = jnp.zeros_like(values[0])
        for slot in range(group):
            total = base
            for other in range(group):
                if other != slot:
                    total = total + values[other] * counts[slot, other]
            refs[slot][at] = total.astype(BF16)


def add_parts(left_ref, right_ref, out_ref):
    out_ref[...] = left_ref[...] + right_ref[...]


def sum_messages(part_ref, *refs):
    messages, out_ref = refs[:-1], refs[-1]
    first = messages[0].shape[0] - 2 * part_ref.shape[0]
    terms = [part_ref[...]] + [join(message, first) for message in messages]
    while len(terms) > 1:
        terms = [terms[i] + terms[i + 1] for i in range(0, len(terms), 2)]
    out_ref[...] = terms[0]


def finish_parts(scale, left_ref, right_ref, out_ref, buffer, sem):
    buffer[...] = (left_ref[...] + right_ref[...]) * scale
    copy = pltpu.make_async_copy(buffer, out_ref, sem.at[0])
    copy.start()
    copy.wait()


def swap(array, axis, bits):
    count = lax.axis_size(axis)
    return lax.ppermute(array, axis, [(i, i ^ bits) for i in range(count)])


def local(queries, key_vectors, value_vectors, out_grad, norm_gain):
    rows, width = queries.shape[1:]
    heads = width // HEAD_DIM
    count = lax.axis_size("seq")
    group = min(4, count)
    steps = int(math.log2(count // group))
    per_slot = heads // (group * CHUNKS)
    per_chunk = heads // CHUNKS
    k, v = ((a.reshape(rows, width), HBM) for a in (key_vectors, value_vectors))
    q, g = ((a.reshape(rows, width), None) for a in (queries, out_grad))
    gain = (norm_gain.reshape(1, width), None)
    me = lax.axis_index("seq")
    cube = 2 * HEAD_DIM**3
    square = HEAD_DIM**2
    columns = per_chunk * HEAD_DIM
    state_shape = (per_slot * HEAD_DIM, HEAD_DIM)
    size = per_slot * square
    thin_state = (state_shape, BF16, VMEM)
    state_outs = [(state_shape, F32, VMEM)] + [thin_state] * (group - 1)
    message = ((state_shape[0] + 2 * heads, HEAD_DIM), BF16, VMEM)
    part_type = ((heads, HEAD_DIM), F32, VMEM)
    carried = steps == 1 and group == 4
    tall = ((rows, columns), BF16, VMEM)
    result = ((rows, width), BF16, HBM)
    sems = pltpu.SemaphoreType.DMA

    def vm(arrays):
        return [(a, VMEM) for a in arrays]

    def spread(states):
        return [states[0]] + [swap(states[slot], "seq", slot) for slot in range(1, group)]

    def across(parts, reverse, name, after, gain_part=None):
        if not steps:
            return None, after
        carry = gain_part is not None
        (total,) = call(
            functools.partial(add_group, group, carry), name, [message if carry else thin_state],
            vm(parts + ([gain_part] if carry else [])), 4 * size, 12 * size, after=after,
        )
        done = [(total, VMEM)]
        if steps == 1:
            got = swap(total, "seq", group)
            return [got, total] if carry else [got], done
        base = None
        for step in range(steps):
            got = swap(total, "seq", group << step).astype(F32)
            upper = (me & (group << step)) != 0
            counts = jnp.logical_not(upper) if reverse else upper
            base = jnp.where(counts, got, 0.0) + (0.0 if base is None else base)
            total = (total.astype(F32) + got).astype(BF16)
        return [base], done

    def scan(parts, base, reverse, name, after, carry=False):
        out = call(
            functools.partial(scan_group, group, reverse, steps, carry), name,
            [thin_state] + [message if carry else thin_state] * (group - 1)
            + ([part_type] if carry else []),
            vm(parts + (base or [])), 16 * size, 20 * size, after=after,
        )
        return spread(out[:group]), [(out[0], VMEM)], out[-1]

    fixed = [(chunk, group, per_slot) for chunk in range(CHUNKS)]
    keys, values, parts, order = [], [], [], []
    for c in range(CHUNKS):
        key, value, *states = call(
            functools.partial(make_states, fixed[c]), f"make_states_{c}",
            [tall, tall] + state_outs, [k, v],
            per_chunk * cube, per_chunk * square * 10, [sems((2, group))] + [VMEM((rows, columns), BF16)] * (0 if c else 2),
            after=order,
        )
        keys.append(key)
        values.append(value)
        parts.append(spread(states))
        order = [(key, VMEM)]

    scores, turned = [], []
    prefixes, normed, back, query_grads = {}, {}, {}, {}
    inner, suffixes, base = {}, {}, {}
    part, results = None, None

    def score(_):
        nonlocal order, scores, turned
        out = call(
            functools.partial(make_scores, fixed[0], CHUNKS), "make_scores", [tall] * (2 * CHUNKS),
            [q] + vm(keys), heads * cube * 2, heads * square * 12, after=order,
        )
        scores, turned = out[:CHUNKS], out[CHUNKS:]
        order = [(turned[0], VMEM)]

    def add_prefix(c):
        nonlocal order
        base[c], order = across(parts[c], False, f"add_prefix_{c}", order)

    def scan_prefix(c):
        nonlocal order
        prefixes[c], order, _ = scan(parts[c], base[c], False, f"scan_prefix_{c}", order)

    def add_suffix(c):
        nonlocal order
        carry = part if carried and c == CHUNKS - 1 else None
        base[c], order = across(back[c], True, f"add_suffix_{c}", order, carry)

    def scan_suffix(c):
        nonlocal order, part
        carry = carried and c == CHUNKS - 1
        suffixes[c], order, out = scan(back[c], base[c], True, f"scan_suffix_{c}", order, carry)
        if carry:
            part = out

    def norm(c):
        nonlocal order, part
        out = call(
            functools.partial(through_norm, fixed[c], part is not None), f"through_norm_{c}",
            [tall, part_type] + state_outs,
            [q, (values[c], VMEM), g, gain]
            + vm([scores[c]] + prefixes[c] + ([] if part is None else [part])),
            per_chunk * cube * 3, per_chunk * square * 14,
            [VMEM((rows, columns), F32)], after=order,
        )
        normed[c], part = out[:2]
        back[c] = spread(out[2:])
        order = [(normed[c], VMEM)]

    def query(c):
        nonlocal order
        wide = ((rows, columns), F32, VMEM)
        query_grads[c], *inner[c] = call(
            functools.partial(query_side, fixed[c]), f"query_side_{c}", [tall, wide, wide],
            [q] + vm([keys[c], values[c], normed[c], turned[c]] + prefixes[c]),
            per_chunk * cube * 6, per_chunk * square * 16,
            [VMEM((rows, columns), BF16)] * 2, after=order,
        )
        order = [(inner[c][0], VMEM)]

    def key(c):
        nonlocal order, results
        has_out = results is not None
        args = vm([keys[c], values[c]] + inner[c] + [query_grads[c]] + suffixes[c])
        results = call(
            functools.partial(key_side, fixed[c], has_out), f"key_side_{c}", [result] * 3,
            args + [(out, HBM) for out in (results if has_out else [])],
            per_chunk * cube * 4, per_chunk * square * 20,
            [VMEM((rows, columns), BF16)] * 2 + [sems((3 * group - 2 + 2 * per_slot,))],
            {len(args) + i: i for i in range(3)} if has_out else None,
            after=() if has_out else order,
        )
        order = [(results[0], HBM)]

    def bits_of(axis):
        return [(axis, 1 << step) for step in range(int(math.log2(lax.axis_size(axis))))]

    hops = bits_of("dp")[1:] + ([] if carried else bits_of("seq")) + bits_of("dp")[:1]
    scale = 1.0 / math.sqrt(count * rows * lax.axis_size("dp"))

    def gain_hop(at):
        nonlocal order, part
        axis, hop = hops[at]
        args = vm([part, swap(part, axis, hop)])
        if at < len(hops) - 1:
            (part,) = call(
                add_parts, f"add_gain_{at}", [part_type], args, width, 12 * width, after=order
            )
            order = [(part, VMEM)]
        else:
            (part,) = call(
                functools.partial(finish_parts, scale), "finish_gain", [(part_type[0], F32, HBM)],
                args, width, 12 * width, [VMEM(part_type[0], F32), sems((1,))],
            )

    def gain_sum(_):
        nonlocal part
        if carried:
            (part,) = call(
                sum_messages, "sum_gain", [part_type], vm([part] + suffixes[CHUNKS - 1][1:]),
                width, 12 * width,
            )

    plan = PLAN
    stages = dict(
        add_prefix=add_prefix, scan_prefix=scan_prefix, add_suffix=add_suffix,
        scan_suffix=scan_suffix, score=score, total=gain_sum, norm=norm, query=query, key=key,
    )
    hop = 0
    for step in plan:
        if step == "gain":
            if hop < len(hops) - 1:
                gain_hop(hop)
                hop += 1
        else:
            stages[step[:-1]](int(step[-1]))
    while hop < len(hops):
        gain_hop(hop)
        hop += 1
    return (*(out.reshape(queries.shape) for out in results), part.reshape(width))


def solution(mesh):
    block = P("dp", "seq", None)
    return jax.shard_map(
        local,
        mesh=mesh,
        in_specs=(block, block, block, block, P()),
        out_specs=(block, block, block, P()),
        check_vma=False,
    )
```

```python
import functools
import math

import jax
import jax.numpy as jnp
from jax import lax
from jax.experimental import pallas as pl
from jax.experimental.pallas import tpu as pltpu
from jax.sharding import PartitionSpec as P

HEAD_DIM = 128
CHUNKS = 2
F32 = jnp.float32
BF16 = jnp.bfloat16
VMEM, HBM = pltpu.VMEM, pltpu.HBM
PLAN = ("add_prefix0", "score0", "add_prefix1", "scan_prefix0", "scan_prefix1", "norm0", "norm1", "add_suffix0", "query0", "gain", "add_suffix1", "scan_suffix0", "scan_suffix1", "query1", "key0", "total0", "key1",
)


def dot(left, right, left_dim, right_dim):
    return lax.dot_general(
        left, right, (((left_dim,), (right_dim,)), ((), ())), preferred_element_type=F32
    )


def call(body, name, outs, args, flops, nbytes, scratch=(), aliases=None, after=()):
    count = len(args)
    args = list(args) + list(after)
    arrays = [
        pltpu.with_memory_space_constraint(array, space) if space else array for array, space in args
    ]

    def kernel(*refs):
        body(*refs[:count], *refs[count + len(after) :])

    return pl.pallas_call(
        kernel,
        name=name,
        out_shape=[space(shape, dtype) for shape, dtype, space in outs],
        in_specs=[pl.BlockSpec(memory_space=space or VMEM) for _, space in args],
        out_specs=[pl.BlockSpec(memory_space=space) for _, _, space in outs],
        scratch_shapes=list(scratch),
        input_output_aliases=aliases or {},
        cost_estimate=pl.CostEstimate(
            flops=int(flops), bytes_accessed=int(nbytes), transcendentals=0
        ),
        compiler_params=pltpu.CompilerParams(vmem_limit_bytes=8 * 2**20),
    )(*arrays)


def place_in(group):
    me = lax.axis_index("seq")
    return lax.rem(me, group), lax.div(me, group)


def slot_columns(place, chunk, slot, per_slot, group, head=0, heads=None):
    owner = jnp.bitwise_xor(place, slot)
    heads = heads or per_slot
    start = ((chunk * group + owner) * per_slot + head) * HEAD_DIM
    return pl.ds(pl.multiple_of(start, heads * HEAD_DIM), heads * HEAD_DIM)


def head_columns(at):
    return pl.ds(at * HEAD_DIM, HEAD_DIM)


def head_rows(at):
    return pl.ds(at * HEAD_DIM, HEAD_DIM), slice(None)


def far_first(group):
    return list(range(group - 1, 0, -1)) + [0]


def load_slots(fixed, place, source, target, sems):
    chunk, group, per_slot = fixed
    width = per_slot * HEAD_DIM
    copies = {}
    for slot in far_first(group):
        copies[slot] = pltpu.make_async_copy(
            source.at[:, slot_columns(place, chunk, slot, per_slot, group)],
            target.at[:, pl.ds(slot * width, width)],
            sems.at[slot],
        )
        copies[slot].start()
    return copies


def store_heads(fixed, place, slot, head, heads, source, target, sem):
    chunk, group, per_slot = fixed
    copy = pltpu.make_async_copy(
        source.at[:, pl.ds((slot * per_slot + head) * HEAD_DIM, heads * HEAD_DIM)],
        target.at[:, slot_columns(place, chunk, slot, per_slot, group, head, heads)],
        sem,
    )
    copy.start()
    return copy


def causal_masks(rows_count):
    rows = lax.broadcasted_iota(jnp.int32, (rows_count, rows_count), 0)
    columns = lax.broadcasted_iota(jnp.int32, (rows_count, rows_count), 1)
    return columns <= rows, rows <= columns


def make_states(fixed, key_in, value_in, key_ref, value_ref, *refs):
    chunk, group, per_slot = fixed
    states, sems = refs[:group], refs[group]
    place, _ = place_in(group)
    if chunk:
        keys = load_slots(fixed, place, key_in, key_ref, sems.at[0])
        values = load_slots(fixed, place, value_in, value_ref, sems.at[1])
    else:
        copies = [
            pltpu.make_async_copy(
                source.at[:, pl.ds(0, buffer.shape[1])], buffer, sems.at[at, 0]
            )
            for at, (source, buffer) in enumerate(zip((key_in, value_in), refs[group + 1 :]))
        ]
        for copy in copies:
            copy.start()
        for copy in copies:
            copy.wait()
    for slot in far_first(group):
        if chunk:
            keys[slot].wait()
            values[slot].wait()
        for head in range(per_slot):
            here = head_columns(slot * per_slot + head)
            if chunk:
                key, value = key_ref[:, here], value_ref[:, here]
            else:
                near = slot_columns(place, 0, slot, per_slot, group, head, 1)
                key, value = (buffer[:, near] for buffer in refs[group + 1 :])
                key_ref[:, here], value_ref[:, here] = key, value
            state = dot(key, value, 0, 0)
            states[slot][head_rows(head)] = state.astype(states[slot].dtype)


def make_scores(fixed, chunks, query_ref, *refs):
    _, group, per_slot = fixed
    place, _ = place_in(group)
    keys, scores, turned = (refs[i * chunks : (i + 1) * chunks] for i in range(3))
    mask, mask_turned = causal_masks(query_ref.shape[0])
    for c in range(chunks):
        for slot in far_first(group):
            for head in range(per_slot):
                here = head_columns(slot * per_slot + head)
                there = slot_columns(place, c, slot, per_slot, group, head, 1)
                query, key = query_ref[:, there], keys[c][:, here]
                scores[c][:, here] = jnp.where(mask, dot(query, key, 1, 1), 0.0).astype(BF16)
                turned[c][:, here] = jnp.where(mask_turned, dot(key, query, 1, 1), 0.0).astype(BF16)


def through_norm(fixed, has_part, query_ref, value_ref, grad_ref, gain_ref, scores_ref, *refs):
    chunk, group, per_slot = fixed
    prefixes, refs = refs[:group], refs[group:]
    if has_part:
        part_in, refs = refs[0], refs[1:]
    attn_ref, part_ref, *refs = refs
    states, attended_ref = refs[:group], refs[group]
    place, _ = place_in(group)
    if has_part:
        before = pl.ds(0, chunk * group * per_slot)
        part_ref[before] = part_in[before]
    each = [(slot, head) for slot in far_first(group) for head in range(per_slot)]
    for slot, head in each:
        here = head_columns(slot * per_slot + head)
        there = slot_columns(place, chunk, slot, per_slot, group, head, 1)
        left = jnp.concatenate([scores_ref[:, here], query_ref[:, there]], axis=1)
        right = jnp.concatenate([value_ref[:, here], prefixes[slot][head_rows(head)]], axis=0)
        attended_ref[:, here] = dot(left, right, 1, 0)
    for slot, head in each:
        here = head_columns(slot * per_slot + head)
        there = slot_columns(place, chunk, slot, per_slot, group, head, 1)
        attended = attended_ref[:, here]
        mean_square = jnp.mean(attended * attended, axis=-1, keepdims=True)
        inv_rms = lax.rsqrt(mean_square + 1e-05)
        normed = attended * inv_rms
        grad_wide = grad_ref[:, there].astype(F32)
        product = grad_wide * normed
        row = (chunk * group + jnp.bitwise_xor(place, slot)) * per_slot + head
        part_ref[pl.ds(row, 1)] = jnp.sum(product, axis=0, keepdims=True)
        gain = gain_ref[:, there]
        mean_product = jnp.mean(product * gain, axis=-1, keepdims=True)
        attn = inv_rms * (grad_wide * gain - normed * mean_product)
        attn_ref[:, here] = attn.astype(BF16)
    for slot, head in each:
        here = head_columns(slot * per_slot + head)
        there = slot_columns(place, chunk, slot, per_slot, group, head, 1)
        state = dot(query_ref[:, there], attn_ref[:, here], 0, 0)
        states[slot][head_rows(head)] = state.astype(states[slot].dtype)


def query_side(fixed, query_ref, key_ref, value_ref, attn_ref, scores_turned_ref, *refs):
    chunk, group, per_slot = fixed
    prefixes, refs = refs[:group], refs[group:]
    out_ref, key_part_ref, value_part_ref, turned_ref, scores_ref = refs
    place, _ = place_in(group)
    mask, mask_turned = causal_masks(key_ref.shape[0])
    for head in range(group * per_slot):
        here = head_columns(head)
        attn, value = attn_ref[:, here], value_ref[:, here]
        scores_ref[:, here] = jnp.where(mask, dot(attn, value, 1, 1), 0.0).astype(BF16)
        turned_ref[:, here] = jnp.where(mask_turned, dot(value, attn, 1, 1), 0.0).astype(BF16)
    for slot in range(group):
        for head in range(per_slot):
            here = head_columns(slot * per_slot + head)
            total = dot(scores_ref[:, here], key_ref[:, here], 1, 0)
            total = total + dot(attn_ref[:, here], prefixes[slot][head_rows(head)], 1, 1)
            out_ref[:, here] = total.astype(BF16)
            there = slot_columns(place, chunk, slot, per_slot, group, head, 1)
            key_part_ref[:, here] = dot(turned_ref[:, here], query_ref[:, there], 1, 0)
            value_part_ref[:, here] = dot(scores_turned_ref[:, here], attn_ref[:, here], 1, 0)


def key_side(
    fixed, has_out, key_ref, value_ref, key_part_ref, value_part_ref, *refs
):
    chunk, group, per_slot = fixed
    suffixes, refs = refs[:group], refs[group:]
    query_grads, refs = ([], refs[3:]) if has_out else (refs[:-6], refs[-6:])
    query_out, key_out, value_out, key_buffer, value_buffer, sems = refs
    place, _ = place_in(group)
    copies = []

    def store(source, target, slot, head, heads, of_chunk=chunk):
        where = (of_chunk, group, per_slot)
        copies.append(
            store_heads(where, place, slot, head, heads, source, target, sems.at[len(copies)])
        )

    for other, query_grad_ref in enumerate(query_grads):
        for slot in range(group):
            store(query_grad_ref, query_out, slot, 0, per_slot, other)
    for slot in range(group):
        for head in range(per_slot):
            here = head_columns(slot * per_slot + head)
            suffix = suffixes[slot][head_rows(head)]
            total = key_part_ref[:, here] + dot(value_ref[:, here], suffix, 1, 1)
            key_buffer[:, here] = total.astype(BF16)
            total = value_part_ref[:, here] + dot(key_ref[:, here], suffix, 1, 0)
            value_buffer[:, here] = total.astype(BF16)
            if slot == group - 1:
                store(key_buffer, key_out, slot, head, 1)
                store(value_buffer, value_out, slot, head, 1)
        if slot < group - 1:
            store(key_buffer, key_out, slot, 0, per_slot)
            store(value_buffer, value_out, slot, 0, per_slot)
    for copy in copies:
        copy.wait()


def split(value):
    high = value.astype(BF16)
    return high, (value - high.astype(F32)).astype(BF16)


def join(ref, first):
    rows = (ref.shape[0] - first) // 2
    return ref[first : first + rows].astype(F32) + ref[first + rows : first + 2 * rows].astype(F32)


def put(ref, first, value):
    rows = value.shape[0]
    ref[first : first + rows], ref[first + rows : first + 2 * rows] = split(value)
    return join(ref, first)


HALF = HEAD_DIM // 2


def pieces(rows):
    return [(pl.ds(row, HALF), slice(None)) for row in range(0, rows, HALF)]


def add_group(group, carry, *refs):
    parts, out_ref = refs[:group], refs[-1]
    rows = parts[0].shape[0]
    for at in pieces(rows):
        total = parts[0][at]
        for slot in range(1, group):
            total = total + parts[slot][at].astype(F32)
        out_ref[at] = total.astype(out_ref.dtype)
    if carry:
        put(out_ref, rows, refs[group][...])


def scan_group(group, reverse, steps, carry, *refs):
    parts, refs = refs[:group], refs[group:]
    rows = parts[0].shape[0]
    if steps:
        base_ref, refs = refs[0], refs[1:]
    if carry:
        sent_ref, part_ref = refs[0], refs[-1]
        refs = refs[1:]
        both = join(sent_ref, rows) + join(base_ref, rows)
        for slot in range(1, group):
            part_ref[...] = put(refs[slot], rows, both)
    place, number = place_in(group)
    use_base = (number == (0 if reverse else 1)).astype(F32)
    counts = {}
    for slot in range(group):
        target = jnp.bitwise_xor(place, slot)
        for other in range(group):
            source = jnp.bitwise_xor(place, other)
            is_before = source > target if reverse else source < target
            counts[slot, other] = is_before.astype(F32)
    for at in pieces(rows):
        values = [part[at].astype(F32) for part in parts]
        if steps:
            base = base_ref[at].astype(F32)
            if steps == 1:
                base = base * use_base
        else:
            base = jnp.zeros_like(values[0])
        for slot in range(group):
            total = base
            for other in range(group):
                if other != slot:
                    total = total + values[other] * counts[slot, other]
            refs[slot][at] = total.astype(BF16)


def add_parts(left_ref, right_ref, out_ref):
    out_ref[...] = left_ref[...] + right_ref[...]


def sum_messages(part_ref, *refs):
    messages, out_ref = refs[:-1], refs[-1]
    first = messages[0].shape[0] - 2 * part_ref.shape[0]
    terms = [part_ref[...]] + [join(message, first) for message in messages]
    while len(terms) > 1:
        terms = [terms[i] + terms[i + 1] for i in range(0, len(terms), 2)]
    out_ref[...] = terms[0]


def finish_parts(scale, left_ref, right_ref, out_ref, buffer, sem):
    buffer[...] = (left_ref[...] + right_ref[...]) * scale
    copy = pltpu.make_async_copy(buffer, out_ref, sem.at[0])
    copy.start()
    copy.wait()


def swap(array, axis, bits):
    count = lax.axis_size(axis)
    return lax.ppermute(array, axis, [(i, i ^ bits) for i in range(count)])


def local(queries, key_vectors, value_vectors, out_grad, norm_gain):
    rows, width = queries.shape[1:]
    heads = width // HEAD_DIM
    count = lax.axis_size("seq")
    group = min(4, count)
    steps = int(math.log2(count // group))
    per_slot = heads // (group * CHUNKS)
    per_chunk = heads // CHUNKS
    k, v = ((a.reshape(rows, width), HBM) for a in (key_vectors, value_vectors))
    q, g = ((a.reshape(rows, width), None) for a in (queries, out_grad))
    gain = (norm_gain.reshape(1, width), None)
    me = lax.axis_index("seq")
    cube = 2 * HEAD_DIM**3
    square = HEAD_DIM**2
    columns = per_chunk * HEAD_DIM
    state_shape = (per_slot * HEAD_DIM, HEAD_DIM)
    size = per_slot * square
    thin_state = (state_shape, BF16, VMEM)
    state_outs = [(state_shape, F32, VMEM)] + [thin_state] * (group - 1)
    message = ((state_shape[0] + 2 * heads, HEAD_DIM), BF16, VMEM)
    part_type = ((heads, HEAD_DIM), F32, VMEM)
    carried = steps == 1 and group == 4
    tall = ((rows, columns), BF16, VMEM)
    result = ((rows, width), BF16, HBM)
    sems = pltpu.SemaphoreType.DMA

    def vm(arrays):
        return [(a, VMEM) for a in arrays]

    def spread(states):
        return [states[0]] + [swap(states[slot], "seq", slot) for slot in range(1, group)]

    def across(parts, reverse, name, after, gain_part=None):
        if not steps:
            return None, after
        carry = gain_part is not None
        (total,) = call(
            functools.partial(add_group, group, carry), name, [message if carry else thin_state],
            vm(parts + ([gain_part] if carry else [])), 4 * size, 12 * size, after=after,
        )
        done = [(total, VMEM)]
        if steps == 1:
            got = swap(total, "seq", group)
            return [got, total] if carry else [got], done
        base = None
        for step in range(steps):
            got = swap(total, "seq", group << step).astype(F32)
            upper = (me & (group << step)) != 0
            counts = jnp.logical_not(upper) if reverse else upper
            base = jnp.where(counts, got, 0.0) + (0.0 if base is None else base)
            total = (total.astype(F32) + got).astype(BF16)
        return [base], done

    def scan(parts, base, reverse, name, after, carry=False):
        out = call(
            functools.partial(scan_group, group, reverse, steps, carry), name,
            [thin_state] + [message if carry else thin_state] * (group - 1)
            + ([part_type] if carry else []),
            vm(parts + (base or [])), 16 * size, 20 * size, after=after,
        )
        return spread(out[:group]), [(out[0], VMEM)], out[-1]

    fixed = [(chunk, group, per_slot) for chunk in range(CHUNKS)]
    keys, values, parts, order = [], [], [], []
    for c in range(CHUNKS):
        key, value, *states = call(
            functools.partial(make_states, fixed[c]), f"make_states_{c}",
            [tall, tall] + state_outs, [k, v],
            per_chunk * cube, per_chunk * square * 10, [sems((2, group))] + [VMEM((rows, columns), BF16)] * (0 if c else 2),
            after=order,
        )
        keys.append(key)
        values.append(value)
        parts.append(spread(states))
        order = [(key, VMEM)]

    scores, turned = [], []
    prefixes, normed, back, query_grads = {}, {}, {}, {}
    inner, suffixes, base = {}, {}, {}
    part, results = None, None

    def score(_):
        nonlocal order, scores, turned
        out = call(
            functools.partial(make_scores, fixed[0], CHUNKS), "make_scores", [tall] * (2 * CHUNKS),
            [q] + vm(keys), heads * cube * 2, heads * square * 12, after=order,
        )
        scores, turned = out[:CHUNKS], out[CHUNKS:]
        order = [(turned[0], VMEM)]

    def add_prefix(c):
        nonlocal order
        base[c], order = across(parts[c], False, f"add_prefix_{c}", order)

    def scan_prefix(c):
        nonlocal order
        prefixes[c], order, _ = scan(parts[c], base[c], False, f"scan_prefix_{c}", order)

    def add_suffix(c):
        nonlocal order
        carry = part if carried and c == CHUNKS - 1 else None
        base[c], order = across(back[c], True, f"add_suffix_{c}", order, carry)

    def scan_suffix(c):
        nonlocal order, part
        carry = carried and c == CHUNKS - 1
        suffixes[c], order, out = scan(back[c], base[c], True, f"scan_suffix_{c}", order, carry)
        if carry:
            part = out

    def norm(c):
        nonlocal order, part
        out = call(
            functools.partial(through_norm, fixed[c], part is not None), f"through_norm_{c}",
            [tall, part_type] + state_outs,
            [q, (values[c], VMEM), g, gain]
            + vm([scores[c]] + prefixes[c] + ([] if part is None else [part])),
            per_chunk * cube * 3, per_chunk * square * 14,
            [VMEM((rows, columns), F32)], after=order,
        )
        normed[c], part = out[:2]
        back[c] = spread(out[2:])
        order = [(normed[c], VMEM)]

    def query(c):
        nonlocal order
        wide = ((rows, columns), F32, VMEM)
        query_grads[c], *inner[c] = call(
            functools.partial(query_side, fixed[c]), f"query_side_{c}", [tall, wide, wide],
            [q] + vm([keys[c], values[c], normed[c], turned[c]] + prefixes[c]),
            per_chunk * cube * 6, per_chunk * square * 16,
            [VMEM((rows, columns), BF16)] * 2, after=order,
        )
        order = [(inner[c][0], VMEM)]

    def key(c):
        nonlocal order, results
        has_out = results is not None
        args = vm([keys[c], values[c]] + inner[c] + suffixes[c])
        if not has_out:
            args += vm([query_grads[chunk] for chunk in range(CHUNKS)])
        results = call(
            functools.partial(key_side, fixed[c], has_out), f"key_side_{c}", [result] * 3,
            args + [(out, HBM) for out in (results if has_out else [])],
            per_chunk * cube * 4, per_chunk * square * 20,
            [VMEM((rows, columns), BF16)] * 2 + [sems(((2 + CHUNKS) * group - 2 + 2 * per_slot,))],
            {len(args) + i: i for i in range(3)} if has_out else None,
            after=() if has_out else order,
        )
        order = [(results[0], HBM)]

    def bits_of(axis):
        return [(axis, 1 << step) for step in range(int(math.log2(lax.axis_size(axis))))]

    hops = bits_of("dp")[1:] + ([] if carried else bits_of("seq")) + bits_of("dp")[:1]
    scale = 1.0 / math.sqrt(count * rows * lax.axis_size("dp"))

    def gain_hop(at):
        nonlocal order, part
        axis, hop = hops[at]
        args = vm([part, swap(part, axis, hop)])
        if at < len(hops) - 1:
            (part,) = call(
                add_parts, f"add_gain_{at}", [part_type], args, width, 12 * width, after=order
            )
            order = [(part, VMEM)]
        else:
            (part,) = call(
                functools.partial(finish_parts, scale), "finish_gain", [(part_type[0], F32, HBM)],
                args, width, 12 * width, [VMEM(part_type[0], F32), sems((1,))],
            )

    def gain_sum(_):
        nonlocal part
        if carried:
            (part,) = call(
                sum_messages, "sum_gain", [part_type], vm([part] + suffixes[CHUNKS - 1][1:]),
                width, 12 * width,
            )

    plan = PLAN
    stages = dict(
        add_prefix=add_prefix, scan_prefix=scan_prefix, add_suffix=add_suffix,
        scan_suffix=scan_suffix, score=score, total=gain_sum, norm=norm, query=query, key=key,
    )
    hop = 0
    for step in plan:
        if step == "gain":
            if hop < len(hops) - 1:
                gain_hop(hop)
                hop += 1
        else:
            stages[step[:-1]](int(step[-1]))
    while hop < len(hops):
        gain_hop(hop)
        hop += 1
    return (*(out.reshape(queries.shape) for out in results), part.reshape(width))


def solution(mesh):
    block = P("dp", "seq", None)
    return jax.shard_map(
        local,
        mesh=mesh,
        in_specs=(block, block, block, block, P()),
        out_specs=(block, block, block, P()),
        check_vma=False,
    )
```
